32 devices in a mesh: dp: 8 (over y, x, core), tp: 4 (over z).
Axes of the slice: x: 2, y: 2, z: 4, core: 2. Of those that a mesh axis runs over, the one named last changes fastest.
Arguments:
- tokens: bfloat16 [16384, 768], P(('dp', 'tp')), may hold values from -6 to 6
- w_qkv: bfloat16 [768, 2304], P('dp', 'tp'), may hold values from -0.21875 to 0.21875
- w_score: bfloat16 [768, 12], P('dp', 'tp'), may hold values from -0.21875 to 0.21875
- w_out: bfloat16 [768, 768], P('tp', 'dp'), may hold values from -0.625 to 0.625
- w_fc: bfloat16 [768, 3072], P('dp', 'tp'), may hold values from -0.21875 to 0.21875
- w_proj: bfloat16 [3072, 768], P('tp', 'dp'), may hold values from -0.15625 to 0.15625
- ln1_gain: bfloat16 [768], P('dp'), may hold values from 0.25 to 1.75
- ln2_gain: bfloat16 [768], P('dp'), may hold values from 0.25 to 1.75
- selected: int32 [256, 12, 64], P('dp', 'tp'), may hold values from 0 to 1023, as said below
- holder: int32 [8], replicated, may hold values from 0 to 1, as said below
- cotangent: bfloat16 [16384, 768], P(('dp', 'tp')), may hold values from -6 to 6
Outputs:
- output: float32 [16384, 768], P(('dp', 'tp'))
- input_grad: float32 [16384, 768], P(('dp', 'tp'))
- grad_qkv: float32 [768, 2304], P('dp', 'tp')
- grad_score: float32 [768, 12], P('dp', 'tp')
- grad_out: float32 [768, 768], P('tp', 'dp')
- grad_fc: float32 [768, 3072], P('dp', 'tp')
- grad_proj: float32 [3072, 768], P('tp', 'dp')
- grad_ln1: float32 [768], P('dp')
- grad_ln2: float32 [768], P('dp')
The draws below stay inside these ranges and needn't reach their ends.
Inputs may be any that keep to these rules, and one draw needn't show every extreme that they name: `selected`: the 64 entries of a row are distinct positions of a prompt. `holder`: in every pair the first two groups have their prompts on different stretches.
All inputs are finite; a program needn't handle non-finite values.
Results may differ from the reference program's by a relative error of at most 0.018.
Values may be sent and summed in bfloat16 or wider, within the bound.
A program may use at most 128 MiB of HBM per device.

```python
import math
import jax
import jax.numpy as jnp
from jax import lax

D = 768
H = 12
HD = 64
FF = 3072
WIN = 64
TOPK = 64
C = 128
NC = 8
P_SIZE = 1024
GPAIR = 2
GROUPS = 8
TOKENS = 16384
N_DP = 8


def draw_selected(key, part):
    key = jax.random.fold_in(key, 3)
    scores = jax.random.randint(key, (TOKENS // WIN, H, P_SIZE), 0, 4096) * P_SIZE + jnp.arange(P_SIZE)
    return lax.top_k(scores, TOPK)[1].astype(jnp.int32)


def draw_holder(key, part):
    key = jax.random.fold_in(key, 5)
    first_key, rest_key = jax.random.split(key)
    pairs = GROUPS // GPAIR
    leading = jax.random.randint(first_key, (pairs, 1), 0, 2)
    others = jax.random.randint(rest_key, (pairs, GPAIR), 0, 2)
    unit = jnp.arange(GPAIR)[None, :]
    table = jnp.where(unit == 0, leading, jnp.where(unit == 1, 1 - leading, others))
    return table.reshape(GROUPS).astype(jnp.int32)


def strengthened(values, own_key, source, target, blocks, factor):
    def block_of(dim):
        return (jnp.arange(values.shape[dim]) // (values.shape[dim] // blocks)).reshape((-1,) + (1,) * (values.ndim - 1 - dim))

    first = jax.random.permutation(own_key, blocks)[block_of(target)]
    second = (block_of(target) + blocks // 2) % blocks
    return jnp.where((block_of(source) == first) | (block_of(source) == second), factor * values, values)


def block_scale(key, shape, cuts, low, top_value):
    factor_of = 1.0
    for dim, blocks in cuts:
        heights = jax.random.uniform(jax.random.fold_in(jax.random.fold_in(key, 6), dim), (blocks,), jnp.float32, low / len(cuts), top_value / len(cuts))
        factor_of = factor_of * jnp.repeat(jnp.exp(heights), shape[dim] // blocks).reshape((-1,) + (1,) * (len(shape) - 1 - dim))
    return factor_of


def centred(rng, dims, scale, limit, shards=(), dtype=jnp.bfloat16):
    values = scale * jax.random.normal(rng, dims, jnp.float32)
    if shards:
        values = values * block_scale(rng, dims, shards, -0.22, 0.18)
    return jnp.clip(values, -limit, limit).astype(dtype)


def bell_draw_with(key, extent, width, reach, shards, heavy, held_as=jnp.bfloat16):
    values = width * jax.random.normal(key, extent, jnp.float32)
    if shards:
        values = values * block_scale(key, extent, shards, -0.22, 0.18)
    return jnp.clip(strengthened(values, jax.random.fold_in(key, 3), *heavy), -reach, reach).astype(held_as)


def setup_inputs(seed: int = 0) -> dict:
    key_list = jax.random.split(jax.random.key(seed), 12)
    return {
        "tokens": centred(key_list[0], (TOKENS, D), 1.0, 6.0, ((0, 32),)),
        "w_qkv": centred(key_list[1], (D, 3 * D), D ** -0.5, 0.21875, ((0, 8), (1, 4))),
        "w_score": centred(key_list[2], (D, H), D ** -0.5, 0.21875, ((0, 8), (1, 4))),
        "w_out": centred(key_list[3], (D, D), (D // 8) ** -0.5, 0.625, ((0, 4), (1, 8))),
        "w_fc": centred(key_list[4], (D, FF), D ** -0.5, 0.21875, ((0, 8), (1, 4))),
        "w_proj": centred(key_list[5], (FF, D), (FF // 2) ** -0.5, 0.15625, ((0, 4), (1, 8))),
        "ln1_gain": jnp.clip(1.0 + 0.15 * jax.random.normal(key_list[6], (D,), jnp.float32), 0.25, 1.75).astype(jnp.bfloat16),
        "ln2_gain": jnp.clip(1.0 + 0.15 * jax.random.normal(key_list[7], (D,), jnp.float32), 0.25, 1.75).astype(jnp.bfloat16),
        "selected": draw_selected(jax.random.fold_in(key_list[11], 71), 0),
        "holder": draw_holder(jax.random.fold_in(key_list[11], 71), 0),
        "cotangent": bell_draw_with(key_list[10], (TOKENS, D), 1.0, 6.0, ((0, 32),), (0, 1, 32, 2.75)),
    }


@jax.custom_vjp
def low(v):
    return lax.optimization_barrier(v.astype(jnp.bfloat16)).astype(jnp.float32)

@jax.custom_vjp
def low_back(v):
    return v

def low_keep(v):
    return (low(v), None)

def low_pass(kept, grad):
    return (grad,)

def back_keep(v):
    return (v, None)

def back_low(kept, grad):
    return (low(grad),)
low.defvjp(low_keep, low_pass)
low_back.defvjp(back_keep, back_low)
EPS = 1e-05
HIGH = lax.Precision.HIGHEST

def matmul(left, right):
    return jnp.dot(left, right, precision=HIGH)

def normalize(rows):
    center = rows - lax.optimization_barrier(jnp.mean(rows, axis=-1, keepdims=True))
    spread = lax.optimization_barrier(jnp.mean(center * center, axis=-1, keepdims=True))
    return center * lax.rsqrt(spread + EPS)

def attend(queries, keys, values, far_keys, far_values, far_gate, chosen, prompt_flags):
    rows = GPAIR * P_SIZE
    blocks = rows // WIN
    scale = 1.0 / math.sqrt(HD)
    position = jnp.arange(rows)
    unit = position // P_SIZE
    segment = unit * (NC + 1) + jnp.where(prompt_flags[unit], NC, position % P_SIZE // C)
    zeros_block = jnp.zeros((WIN, H, HD), jnp.float32)

    def framed(table):
        earlier = jnp.concatenate([zeros_block, table[:-WIN]], 0).reshape(blocks, WIN, H, HD)
        return jnp.concatenate([earlier, table.reshape(blocks, WIN, H, HD)], 1)
    block_keys = framed(keys)
    block_values = framed(values)
    block_queries = queries.reshape(blocks, WIN, H, HD)
    near = jnp.einsum('bqhd,bkhd->bhqk', block_queries, block_keys, precision=HIGH) * scale
    query_pos = position.reshape(blocks, WIN)
    key_pos = query_pos[:, :1] - WIN + jnp.arange(2 * WIN)[None, :]
    distance = query_pos[:, :, None] - key_pos[:, None, :]
    key_seg = segment[jnp.clip(key_pos, 0, rows - 1)]
    near_ok = (distance >= 0) & (distance < WIN) & (key_pos[:, None, :] >= 0)
    near_ok = near_ok & (key_seg[:, None, :] == segment.reshape(blocks, WIN)[:, :, None])
    block_unit = jnp.arange(blocks) * WIN // P_SIZE
    picked = block_unit[:, None, None] * P_SIZE + chosen
    head_ids = jnp.arange(H)[None, :, None]
    sel_keys = far_keys[picked, head_ids]
    sel_values = far_values[picked, head_ids]
    sel_gate = far_gate[picked, head_ids]
    far = jnp.einsum('bqhd,bhtd->bhqt', block_queries, sel_keys, precision=HIGH) * scale + sel_gate[:, :, None, :]
    far_ok = jnp.logical_not(prompt_flags[block_unit])
    logits = low_back(jnp.concatenate([near, far], -1))
    valid = jnp.concatenate([jnp.broadcast_to(near_ok[:, None], near.shape), jnp.broadcast_to(far_ok[:, None, None, None], far.shape)], -1)
    top = lax.optimization_barrier(jnp.max(jnp.where(valid, logits, -1e+30), -1, keepdims=True))
    raised = jnp.exp(jnp.where(valid, logits - top, -1e+30))
    shares = low(raised / lax.optimization_barrier(jnp.sum(raised, -1, keepdims=True)))
    result = jnp.einsum('bhqk,bkhd->bqhd', shares[..., :2 * WIN], block_values, precision=HIGH)
    result = result + jnp.einsum('bhqt,bhtd->bqhd', shares[..., 2 * WIN:], sel_values, precision=HIGH)
    return result.reshape(rows, H * HD)

def layer(stream, w_qkv, w_score, w_out, w_fc, w_proj, ln1_gain, ln2_gain, chosen, holds):
    rows = GPAIR * P_SIZE
    first = low(normalize(stream) * ln1_gain)
    mixed = low(low_back(matmul(first, w_qkv))).reshape(2, rows, H, 3, HD)
    queries = mixed[:, :, :, 0]
    keys = mixed[:, :, :, 1]
    values = mixed[:, :, :, 2]
    gate = low(jax.nn.log_sigmoid(low_back(matmul(first, w_score)))).reshape(2, rows, H)
    chosen_two = chosen.reshape(2, rows // WIN, H, TOPK)
    flags = jnp.stack([holds == 0, holds == 1])
    attended = jax.vmap(attend)(queries, keys, values, keys[::-1], values[::-1], gate[::-1], chosen_two, flags)
    attended = low(low_back(attended.reshape(2 * rows, D)))
    resid = stream + low_back(matmul(attended, w_out))
    second = low(normalize(resid) * ln2_gain)
    hidden = low(jax.nn.gelu(low_back(matmul(second, w_fc))))
    return resid + low_back(matmul(hidden, w_proj))

def reference(tokens, w_qkv, w_score, w_out, w_fc, w_proj, ln1_gain, ln2_gain, selected, holder, cotangent):
    params = tuple((item.astype(jnp.float32) for item in (w_qkv, w_score, w_out, w_fc, w_proj, ln1_gain, ln2_gain)))
    rows = GPAIR * P_SIZE
    pairs = N_DP // 2
    streams = tokens.astype(jnp.float32).reshape(pairs, 2 * rows, D)
    upstreams = cotangent.astype(jnp.float32).reshape(pairs, 2 * rows, D)
    chosen_all = selected.reshape(pairs, 2 * rows // WIN, H, TOPK)
    holds_all = holder.reshape(pairs, GPAIR)

    def one_pair(totals, inputs):
        stream, upstream, chosen, holds = inputs

        def forward(stream_in, *weights):
            return layer(stream_in, *weights, chosen, holds)
        result, pull = jax.vjp(forward, stream, *params)
        back = pull(upstream)
        return (tuple((total + extra for total, extra in zip(totals, back[1:]))), (result, back[0]))
    zeros_all = tuple((jnp.zeros_like(item) for item in params))
    totals, (results, grads) = lax.scan(one_pair, zeros_all, (streams, upstreams, chosen_all, holds_all))
    return (results.reshape(TOKENS, D), grads.reshape(TOKENS, D), totals[0], totals[1], totals[2], totals[3], totals[4], totals[5], totals[6])
```

```python
import functools
import math

import jax
import jax.numpy as jnp
from jax import lax
from jax.experimental import pallas as pl
from jax.experimental.pallas import tpu as pltpu
from jax.sharding import PartitionSpec as P

HD = 64
WIN = 64
TOPK = 64
C = 128
NC = 8
P_SIZE = 1024
GPAIR = 2


EPS = 1e-05


def swapped(array, axis, stride):
    return lax.ppermute(array, axis, [(i, i ^ 1 << stride) for i in range(lax.axis_size(axis))])


def product(left, right):
    return jnp.dot(left, right, preferred_element_type=jnp.float32)


def times_trans(left, right):
    return lax.dot_general(
        left, right, (((1,), (1,)), ((), ())), preferred_element_type=jnp.float32
    )


def trans_times(left, right):
    return lax.dot_general(
        left, right, (((0,), (0,)), ((), ())), preferred_element_type=jnp.float32
    )


def normalize(rows):
    center = rows - jnp.mean(rows, axis=-1, keepdims=True)
    spread = jnp.mean(center * center, axis=-1, keepdims=True)
    inverse = lax.rsqrt(spread + EPS)
    return (center * inverse, inverse)


def norm_back(grad_in, normed, inverse, gain):
    inner = grad_in * gain
    return inverse * (
        inner
        - jnp.mean(inner, -1, keepdims=True)
        - normed * jnp.mean(inner * normed, -1, keepdims=True)
    )


MESH = pl.DeviceIdType.MESH
COLS = (640, 256, 768, 768)
OFF = (0, 640, 896, 1664)
WIDE = 2432
TP = 4

class Place:
    def __init__(self, inner):
        self.inner = inner
        self.dp = lax.axis_index("dp")
        self.z = lax.axis_index("tp")
        self.k = self.dp // inner
        self.cb = self.k % 2
        self.yx = self.k // 2
        self.step = inner
        self.core = (self.flip(1), self.z)
        self.xn = (self.flip(2), self.z)
        self.yn = (self.flip(4), self.z)
    def flip(self, bit):
        d = self.k // bit % 2
        return self.dp + (1 - 2 * d) * bit * self.inner
    def zdev(self, s):
        return (self.dp, (self.z + s) % TP)

def barrier(devs):
    b = pltpu.get_barrier_semaphore()
    for d in devs:
        pl.semaphore_signal(b, inc=1, device_id=d, device_id_type=MESH)
    pl.semaphore_wait(b, len(devs))

class Gather:
    def __init__(self, at, own, bufs, sems):
        self.at, self.own, self.bufs = at, own, bufs
        self.zs, self.zr, self.ps, self.pr = sems
    def put(self, src, dst, ssem, rsem, dev):
        return pltpu.make_async_remote_copy(src_ref=src, dst_ref=dst, send_sem=ssem, recv_sem=rsem, device_id=dev, device_id_type=MESH)
    def slot(self, s):
        return (self.at.z - s + TP) % TP
    def c_z(self, p, s):
        a = self.at
        return self.put(self.own[p], self.bufs[p].at[a.z, a.yx, a.cb], self.zs.at[p, s-1], self.zr.at[p, s-1], a.zdev(s))
    def c_xy(self, p, s, j):
        a = self.at
        r = self.bufs[p].at[self.slot(s), a.yx, a.cb]
        return self.put(r, r, self.ps.at[p, s, j], self.pr.at[p, s, j], (a.xn, a.yn)[j])
    def c_half(self, p, s, j):
        a = self.at
        h = self.bufs[p].shape[3] // 2
        other = a.yx + (1 - 2 * (a.yx % 2)) if j == 0 else a.yx + (1 - 2 * (a.yx // 2)) * 2
        r = self.bufs[p].at[self.slot(s), other, a.cb, pl.ds(j * h, h)]
        return self.put(r, r, self.ps.at[p, s, 2 + j], self.pr.at[p, s, 2 + j], (a.yn, a.xn)[j])
    def c_core(self, p, s):
        a = self.at
        r = self.bufs[p].at[self.slot(s), :, a.cb]
        return self.put(r, r, self.ps.at[p, s, 4], self.pr.at[p, s, 4], a.core)
    def start_z(self, p):
        for s in (1, 2, 3):
            self.c_z(p, s).start()
    def st1(self, p, s):
        if s:
            self.c_z(p, s).wait_recv()
        for j in (0, 1):
            self.c_xy(p, s, j).start()
    def st2(self, p, s):
        for j in (0, 1):
            self.c_xy(p, s, j).wait_recv()
            self.c_half(p, s, j).start()
    def st3(self, p, s):
        for j in (0, 1):
            self.c_half(p, s, j).wait_recv()
        self.c_core(p, s).start()
    def st4(self, p, s):
        self.c_core(p, s).wait_recv()
    def drain(self, p):
        for s in (1, 2, 3):
            self.c_z(p, s).wait_send()
        for s in range(4):
            for j in (0, 1):
                self.c_xy(p, s, j).wait_send()
                self.c_half(p, s, j).wait_send()
            self.c_core(p, s).wait_send()

def gather_kernel(inner, w_ref, oa, ob, oc, od, ga, gb, gc, gd, zs, zr, ps, pr, ls):
    at = Place(inner)
    bufs = (ga, gb, gc, gd)
    barrier([at.core, at.xn, at.yn] + [at.zdev(s) for s in (1, 2, 3)])
    own = [w_ref.at[:, pl.ds(OFF[p], COLS[p])] for p in range(4)]
    g = Gather(at, own, bufs, (zs, zr, ps, pr))
    g.start_z(0)
    for p in range(4):
        bufs[p][at.z, at.yx, at.cb] = own[p][...]
    seq = [(p, s) for p in range(4) for s in range(4)]
    n = len(seq)
    for i in range(-1, n + 3):
        if i >= 0 and i % 4 == 0 and i // 4 + 1 < 4:
            g.start_z(i // 4 + 1)
        if i + 1 < n:
            g.st1(*seq[i + 1])
        if 0 <= i - 1 < n:
            g.st2(*seq[i - 1])
        if 0 <= i - 2 < n:
            g.st3(*seq[i - 2])
        if 0 <= i - 3 < n:
            g.st4(*seq[i - 3])
    for p in range(4):
        g.drain(p)
    copies = [pltpu.make_async_copy(b, o, ls.at[p]) for p, (b, o) in enumerate(zip(bufs, (oa, ob, oc, od)))]
    for copy in copies:
        copy.start()
    for copy in copies:
        copy.wait()


def gathered(pack, inner):
    dma = pltpu.SemaphoreType.DMA
    return pl.pallas_call(
        functools.partial(gather_kernel, inner),
        out_shape=[jax.ShapeDtypeStruct((TP, 4, 2, 96, c), jnp.bfloat16) for c in COLS],
        in_specs=[pl.BlockSpec(memory_space=pltpu.VMEM)],
        out_specs=[pl.BlockSpec(memory_space=pl.ANY)] * 4,
        scratch_shapes=[pltpu.VMEM((TP, 4, 2, 96, c), jnp.bfloat16) for c in COLS]
        + [dma((4, 3)), dma((4, 3)), dma((4, 4, 5)), dma((4, 4, 5)), dma((4,))],
        compiler_params=pltpu.CompilerParams(
            collective_id=0, has_side_effects=True, vmem_limit_bytes=40 << 20
        ),
    )(pack)


def per_device(
    tokens, w_qkv, w_score, w_out, w_fc, w_proj, ln1_gain, ln2_gain, selected, holder, cotangent
):
    inner = lax.axis_size("dp") // 8
    gains = jnp.stack([ln1_gain, ln2_gain], axis=1)
    pack = jnp.concatenate(
        [w_qkv, w_score, gains, jnp.zeros((w_qkv.shape[0], 59), jnp.bfloat16), w_out.T, jnp.zeros((w_qkv.shape[0], 64), jnp.bfloat16), w_fc, w_proj.T],
        axis=1,
    )
    if inner > 1:
        groups = [[o * inner + i for i in range(inner)] for o in range(8)]
        pack = lax.all_gather(pack, "dp", axis=0, tiled=True, axis_index_groups=groups)
    here = [
        lax.dynamic_index_in_dim(g, lax.axis_index("tp"), 0, False).reshape(768, -1)
        for g in gathered(pack, inner)
    ]
    whole_qkv, whole_score = here[0][:, :576], here[0][:, 576:579]
    gain_one, gain_two = here[0][:, 579], here[0][:, 580]
    whole_out, whole_fc, whole_proj = here[1][:, :192].T, here[2], here[3].T
    parts = lax.axis_size("tp")
    local_rows = tokens.shape[0]
    rows = local_rows * parts
    heads = whole_score.shape[1]
    blocks = rows // WIN
    scale = 1.0 / math.sqrt(HD)
    side = lax.axis_index("dp") % 2
    pair_index = lax.axis_index("dp") // 2
    holds = lax.dynamic_slice_in_dim(holder, pair_index * GPAIR, GPAIR, 0)
    prompt_flag = (holds == side).astype(jnp.int32)
    stream = tokens.astype(jnp.float32)
    normed_one, inverse_one = normalize(stream)
    first_low = (normed_one * gain_one.astype(jnp.float32)).astype(jnp.bfloat16)
    first_full = lax.all_gather(first_low, "tp", axis=0, tiled=True)
    mixed = product(first_full, whole_qkv).astype(jnp.bfloat16).reshape(rows, heads, 3, HD)
    queries = mixed[:, :, 0]
    keys_near = mixed[:, :, 1]
    values_near = mixed[:, :, 2]
    raw_gate = product(first_full, whole_score)
    gate_low = jax.nn.log_sigmoid(raw_gate).astype(jnp.bfloat16)
    far_keys, far_values, far_gate = swapped((keys_near, values_near, gate_low), "dp", 0)
    position = jnp.arange(rows)
    unit = position // P_SIZE
    unit_prompt = (
        jnp.sum(
            jnp.where(unit[:, None] == jnp.arange(GPAIR)[None, :], prompt_flag[None, :], 0), axis=1
        )
        > 0
    )
    segment = unit * (NC + 1) + jnp.where(unit_prompt, NC, position % P_SIZE // C)
    query_pos = position.reshape(blocks, WIN)
    key_pos = query_pos[:, :1] - WIN + jnp.arange(2 * WIN)[None, :]
    distance = query_pos[:, :, None] - key_pos[:, None, :]
    query_seg = segment.reshape(blocks, WIN)
    earlier_seg = jnp.concatenate([jnp.full((WIN,), -1, jnp.int32), segment[:-WIN]]).reshape(
        blocks, WIN
    )
    key_seg = jnp.concatenate([earlier_seg, query_seg], 1)
    near_ok = (distance >= 0) & (distance < WIN) & (key_seg[:, None, :] == query_seg[:, :, None])
    block_unit = jnp.arange(blocks) * WIN // P_SIZE
    far_ok = jnp.logical_not(unit_prompt.reshape(blocks, WIN)[:, 0])
    picked = (
        (block_unit[:, None, None] * P_SIZE + selected)
        .transpose(1, 0, 2)
        .reshape(heads, blocks * TOPK)
    )

    def pick(table):
        gathered = jnp.take_along_axis(table.transpose(1, 0, 2), picked[:, :, None], axis=1)
        return gathered.reshape(heads, blocks, TOPK, HD)

    sel_keys = pick(far_keys)
    sel_values = pick(far_values)
    sel_gate = (
        jnp.take_along_axis(far_gate.T, picked, axis=1)
        .reshape(heads, blocks, TOPK)
        .astype(jnp.float32)
    )

    def framed(table):
        earlier = jnp.concatenate(
            [jnp.zeros((WIN, heads, HD), table.dtype), table[:-WIN]], 0
        ).reshape(blocks, WIN, heads, HD)
        return jnp.concatenate([earlier, table.reshape(blocks, WIN, heads, HD)], 1)

    block_keys = framed(keys_near)
    block_values = framed(values_near)
    block_queries = queries.reshape(blocks, WIN, heads, HD)
    near = (
        jnp.einsum("bqhd,bkhd->bhqk", block_queries, block_keys, preferred_element_type=jnp.float32)
        * scale
    )
    far = (
        jnp.einsum("bqhd,hbtd->bhqt", block_queries, sel_keys, preferred_element_type=jnp.float32)
        * scale
    )
    far = far + sel_gate.transpose(1, 0, 2)[:, :, None, :]
    logits = jnp.concatenate([near, far], -1)
    valid = jnp.concatenate(
        [
            jnp.broadcast_to(near_ok[:, None], near.shape),
            jnp.broadcast_to(far_ok[:, None, None, None], far.shape),
        ],
        -1,
    )
    top = jnp.max(jnp.where(valid, logits, -1e30), -1, keepdims=True)
    raised = jnp.exp(jnp.where(valid, logits - top, -1e30))
    shares = raised / jnp.sum(raised, -1, keepdims=True)
    shares_low = shares.astype(jnp.bfloat16)
    attended = jnp.einsum(
        "bhqk,bkhd->bqhd",
        shares_low[..., : 2 * WIN],
        block_values,
        preferred_element_type=jnp.float32,
    )
    attended = attended + jnp.einsum(
        "bhqt,hbtd->bqhd",
        shares_low[..., 2 * WIN :],
        sel_values,
        preferred_element_type=jnp.float32,
    )
    attended = attended.reshape(rows, heads * HD).astype(jnp.bfloat16)
    branch = lax.psum_scatter(
        product(attended, whole_out).astype(jnp.bfloat16), "tp", scatter_dimension=0, tiled=True
    ).astype(jnp.float32)
    resid = stream + branch
    normed_two, inverse_two = normalize(resid)
    second_low = (normed_two * gain_two.astype(jnp.float32)).astype(jnp.bfloat16)
    second_full = lax.all_gather(second_low, "tp", axis=0, tiled=True)
    pre_act = product(second_full, whole_fc)
    hidden = jax.nn.gelu(pre_act).astype(jnp.bfloat16)
    output = resid + lax.psum_scatter(
        product(hidden, whole_proj).astype(jnp.bfloat16), "tp", scatter_dimension=0, tiled=True
    ).astype(jnp.float32)
    upstream_full = lax.all_gather(cotangent, "tp", axis=0, tiled=True)
    grad_proj = trans_times(hidden, upstream_full)
    grad_hidden = times_trans(upstream_full, whole_proj)
    grad_pre = jax.vjp(jax.nn.gelu, pre_act)[1](grad_hidden)[0].astype(jnp.bfloat16)
    grad_fc = trans_times(second_full, grad_pre)
    grad_second = lax.psum_scatter(
        times_trans(grad_pre, whole_fc), "tp", scatter_dimension=0, tiled=True
    )
    ln2_part = jnp.sum(grad_second * normed_two, 0)
    grad_resid = cotangent.astype(jnp.float32) + norm_back(
        grad_second, normed_two, inverse_two, gain_two.astype(jnp.float32)
    )
    branch_full = lax.all_gather(grad_resid.astype(jnp.bfloat16), "tp", axis=0, tiled=True)
    grad_out = trans_times(attended, branch_full)
    grad_att = (
        times_trans(branch_full, whole_out).astype(jnp.bfloat16).reshape(blocks, WIN, heads, HD)
    )
    grad_near = jnp.einsum(
        "bqhd,bkhd->bhqk", grad_att, block_values, preferred_element_type=jnp.float32
    )
    grad_far = jnp.einsum(
        "bqhd,hbtd->bhqt", grad_att, sel_values, preferred_element_type=jnp.float32
    )
    grad_shares = jnp.concatenate([grad_near, grad_far], -1)
    grad_logits = (
        shares * (grad_shares - jnp.sum(shares * grad_shares, -1, keepdims=True))
    ).astype(jnp.bfloat16)
    logit_near = grad_logits[..., : 2 * WIN]
    logit_far = grad_logits[..., 2 * WIN :]
    grad_queries = jnp.einsum(
        "bhqk,bkhd->bqhd", logit_near, block_keys, preferred_element_type=jnp.float32
    )
    grad_queries = grad_queries + jnp.einsum(
        "bhqt,hbtd->bqhd", logit_far, sel_keys, preferred_element_type=jnp.float32
    )
    grad_queries = (grad_queries * scale).reshape(rows, heads, HD).astype(jnp.bfloat16)
    grad_block_keys = (
        jnp.einsum("bhqk,bqhd->bkhd", logit_near, block_queries, preferred_element_type=jnp.float32)
        * scale
    )
    grad_block_values = jnp.einsum(
        "bhqk,bqhd->bkhd", shares_low[..., : 2 * WIN], grad_att, preferred_element_type=jnp.float32
    )

    def unframe(grads):
        earlier = grads[:, :WIN].reshape(rows, heads, HD)
        own_part = grads[:, WIN:].reshape(rows, heads, HD)
        return own_part + jnp.concatenate(
            [earlier[WIN:], jnp.zeros((WIN, heads, HD), jnp.float32)], 0
        )

    near_dkeys = unframe(grad_block_keys)
    near_dvalues = unframe(grad_block_values)
    sel_dkeys = (
        jnp.einsum("bhqt,bqhd->hbtd", logit_far, block_queries, preferred_element_type=jnp.float32)
        * scale
    )
    sel_dvalues = jnp.einsum(
        "bhqt,bqhd->hbtd", shares_low[..., 2 * WIN :], grad_att, preferred_element_type=jnp.float32
    )
    sel_dgate = jnp.sum(logit_far.astype(jnp.float32), axis=2).transpose(1, 0, 2)
    flat_index = (jnp.arange(heads)[:, None] * rows + picked).reshape(-1)

    def place(entries, width):
        spread_out = (
            jnp.zeros((heads * rows, width), jnp.float32)
            .at[flat_index]
            .add(entries.reshape(heads * blocks * TOPK, width))
        )
        return spread_out.reshape(heads, rows, width).transpose(1, 0, 2)

    far_dkeys = place(sel_dkeys, HD)
    far_dvalues = place(sel_dvalues, HD)
    far_dgate = place(sel_dgate[..., None], 1)[:, :, 0]
    back_keys, back_values, back_gate = (
        swapped(far_dkeys.astype(jnp.bfloat16), "dp", 0).astype(far_dkeys.dtype),
        swapped(far_dvalues.astype(jnp.bfloat16), "dp", 0).astype(far_dvalues.dtype),
        swapped(far_dgate.astype(jnp.bfloat16), "dp", 0).astype(far_dgate.dtype),
    )
    grad_keys = (near_dkeys + back_keys).astype(jnp.bfloat16)
    grad_values = (near_dvalues + back_values).astype(jnp.bfloat16)
    grad_raw = (back_gate * jax.nn.sigmoid(-raw_gate)).astype(jnp.bfloat16)
    grad_mixed = jnp.stack([grad_queries, grad_keys, grad_values], axis=2).reshape(
        rows, 3 * heads * HD
    )
    grad_qkv = trans_times(first_full, grad_mixed)
    grad_score = trans_times(first_full, grad_raw)
    grad_first = lax.psum_scatter(
        (times_trans(grad_mixed, whole_qkv) + times_trans(grad_raw, whole_score)).astype(
            jnp.bfloat16
        ),
        "tp",
        scatter_dimension=0,
        tiled=True,
    ).astype(jnp.float32)
    ln1_part = jnp.sum(grad_first * normed_one, 0)
    input_grad = grad_resid + norm_back(
        grad_first, normed_one, inverse_one, gain_one.astype(jnp.float32)
    )
    ln1_total, ln2_total = lax.psum((ln1_part, ln2_part), "tp")
    reduced = (
        lax.psum_scatter(grad_qkv, "dp", scatter_dimension=0, tiled=True),
        lax.psum_scatter(grad_score, "dp", scatter_dimension=0, tiled=True),
        lax.psum_scatter(grad_out, "dp", scatter_dimension=1, tiled=True),
        lax.psum_scatter(grad_fc, "dp", scatter_dimension=0, tiled=True),
        lax.psum_scatter(grad_proj, "dp", scatter_dimension=1, tiled=True),
        lax.psum_scatter(ln1_total, "dp", scatter_dimension=0, tiled=True),
        lax.psum_scatter(ln2_total, "dp", scatter_dimension=0, tiled=True),
    )
    return (
        output,
        input_grad,
        reduced[0],
        reduced[1],
        reduced[2],
        reduced[3],
        reduced[4],
        reduced[5],
        reduced[6],
    )


def solution(mesh):
    in_specs = (
        P(("dp", "tp"), None),
        P("dp", "tp"),
        P("dp", "tp"),
        P("tp", "dp"),
        P("dp", "tp"),
        P("tp", "dp"),
        P("dp"),
        P("dp"),
        P("dp", "tp", None),
        P(),
        P(("dp", "tp"), None),
    )
    out_specs = (
        P(("dp", "tp"), None),
        P(("dp", "tp"), None),
        P("dp", "tp"),
        P("dp", "tp"),
        P("tp", "dp"),
        P("dp", "tp"),
        P("tp", "dp"),
        P("dp"),
        P("dp"),
    )
    return jax.shard_map(
        per_device, mesh=mesh, in_specs=in_specs, out_specs=out_specs, check_vma=False
    )
```

```python
import functools
import math

import jax
import jax.numpy as jnp
from jax import lax
from jax.experimental import pallas as pl
from jax.experimental.pallas import tpu as pltpu
from jax.sharding import PartitionSpec as P

MESH = pl.DeviceIdType.MESH
BF = jnp.bfloat16
F32 = jnp.float32
D = 768
HD = 64
COLS = (640, 256, 768, 768)
OFF = (0, 640, 896, 1664)
WIDE = 2432
TP = 4
ROWS = 512
UNIT = 1024
TILE = 128
EPS = 1e-05
FAR_OFF = -1e30
GELU = 0.7978845608
CUBE = 0.044715
SLOTS = 5


def nn(left, right):
    return jnp.dot(left, right, preferred_element_type=F32)


def nt(left, right):
    return lax.dot_general(left, right, (((1,), (1,)), ((), ())), preferred_element_type=F32)


def tn(left, right):
    return lax.dot_general(left, right, (((0,), (0,)), ((), ())), preferred_element_type=F32)


class Place:
    def __init__(self, inner):
        self.inner = inner
        self.dp = lax.axis_index("dp")
        self.z = lax.axis_index("tp")
        self.k = self.dp // inner
        self.cb = self.k % 2
        self.yx = self.k // 2
        self.core = (self.flip(1), self.z)
        self.xn = (self.flip(2), self.z)
        self.yn = (self.flip(4), self.z)
        self.c = self.dp % 2
        self.pair = (self.dp + 1 - 2 * self.c, self.z)
        self.half = self.z % 2
        self.zp = (self.dp, self.z + 1 - 2 * self.half)
        self.x_yx = self.yx + 1 - 2 * (self.yx % 2)
        self.y_yx = self.yx + 2 - 4 * (self.yx // 2)
        self.d_yx = 3 - self.yx

    def flip(self, bit):
        on = self.k // bit % 2
        return self.dp + (1 - 2 * on) * bit * self.inner

    def zdev(self, s):
        return (self.dp, (self.z + s) % TP)

    def barrier(self):
        devices = [self.core, self.xn, self.yn] + [self.zdev(s) for s in (1, 2, 3)]
        if self.inner > 1:
            devices.append(self.pair)
        sem = pltpu.get_barrier_semaphore()
        for device in devices:
            pl.semaphore_signal(sem, inc=1, device_id=device, device_id_type=MESH)
        pl.semaphore_wait(sem, len(devices))


def put(src, dst, send, recv, device):
    return pltpu.make_async_remote_copy(
        src_ref=src, dst_ref=dst, send_sem=send, recv_sem=recv, device_id=device, device_id_type=MESH
    )


class Gather:
    def __init__(self, at, own, bufs, sems):
        self.at, self.own, self.bufs = at, own, bufs
        self.zs, self.zr, self.ps, self.pr = sems
        self.order = [(p, s) for p in range(4) for s in range(4)]
        self.now = -1

    def slot(self, s):
        return (self.at.z - s + TP) % TP

    def along_z(self, p, s):
        a = self.at
        return put(
            self.own[p], self.bufs[p].at[a.z, a.yx, a.cb], self.zs.at[p, s - 1], self.zr.at[p, s - 1], a.zdev(s)
        )

    def along_xy(self, p, s, j):
        a = self.at
        ref = self.bufs[p].at[self.slot(s), a.yx, a.cb]
        return put(ref, ref, self.ps.at[p, s, j], self.pr.at[p, s, j], (a.xn, a.yn)[j])

    def forward(self, p, s, j):
        a = self.at
        ref = self.bufs[p].at[self.slot(s), (a.x_yx, a.y_yx)[j], a.cb, pl.ds(j * 48, 48)]
        return put(ref, ref, self.ps.at[p, s, 2 + j], self.pr.at[p, s, 2 + j], (a.yn, a.xn)[j])

    def to_core(self, p, s):
        a = self.at
        ref = self.bufs[p].at[self.slot(s), :, a.cb]
        return put(ref, ref, self.ps.at[p, s, 4], self.pr.at[p, s, 4], a.core)

    def start_z(self, p):
        for s in (1, 2, 3):
            self.along_z(p, s).start()

    def tick(self):
        i, n = self.now, len(self.order)
        self.now += 1
        if i >= 0 and i % 4 == 0 and i // 4 + 1 < 4:
            self.start_z(i // 4 + 1)
        if i + 1 < n:
            p, s = self.order[i + 1]
            if s:
                self.along_z(p, s).wait_recv()
            for j in (0, 1):
                self.along_xy(p, s, j).start()
        if 0 <= i - 1 < n:
            p, s = self.order[i - 1]
            for j in (0, 1):
                self.along_xy(p, s, j).wait_recv()
                self.forward(p, s, j).start()
        if 0 <= i - 2 < n:
            p, s = self.order[i - 2]
            for j in (0, 1):
                self.forward(p, s, j).wait_recv()
            self.to_core(p, s).start()
        if 0 <= i - 3 < n:
            self.to_core(*self.order[i - 3]).wait_recv()

    def ready(self, p, s):
        while self.now <= self.order.index((p, s)) + 3:
            self.tick()

    def drain(self):
        self.ready(3, 3)
        for p, s in self.order:
            if s:
                self.along_z(p, s).wait_send()
            for j in (0, 1):
                self.along_xy(p, s, j).wait_send()
                self.forward(p, s, j).wait_send()
            self.to_core(p, s).wait_send()


def layer_norm(rows):
    center = rows - jnp.mean(rows, axis=-1, keepdims=True)
    spread = jnp.mean(center * center, axis=-1, keepdims=True)
    inverse = lax.rsqrt(spread + EPS)
    return center * inverse, inverse


def lanes(shape):
    return lax.broadcasted_iota(jnp.int32, shape, len(shape) - 1)


def halves(shape):
    return lanes(shape) < HD


def only(tile, left):
    keep = halves(tile.shape)
    return jnp.where(keep if left else jnp.logical_not(keep), tile.astype(F32), 0.0).astype(tile.dtype)


def gate_lane(head):
    return head if head < 3 else HD + head - 3


def forward_kernel(
    inner, tok, pack, sel, flag,
    out, resid_o, gains_o, hid_o, dg_o, att_o, pt_o, kvp_o, kvc_o, qp_o, qc_o, sb_o, sr_o, sg_o, first_o, ga_o, gw_o, gc_o, gd_o,
    ga, gb, gc, gd, first, mixed, mrecv, sg, selz, selp, selrow, selcol, kvp, kvc, qp, qc, gp, sb, oh, bias, pt, atp, atc,
    att, resid, second, hid, dg, gwt, gains,
    zs, zr, ps, pr, es, er, ls,
):
    at = Place(inner)
    bufs = (ga, gb, gc, gd)
    own = [pack.at[:, pl.ds(OFF[p], COLS[p])] for p in range(4)]
    g = Gather(at, own, bufs, (zs, zr, ps, pr))
    saved = []

    def save(src, dst):
        copy = pltpu.make_async_copy(src, dst, ls.at[len(saved)])
        copy.start()
        saved.append(copy)

    at.barrier()
    g.start_z(0)
    for p in range(4):
        bufs[p][at.z, at.yx, at.cb] = own[p][...]
    g.tick()

    selz[at.z] = sel[at.z]
    sel_out = [
        put(sel.at[(at.z + s) % TP], selz.at[at.z], es.at[s - 1], er.at[s - 1], at.zdev(s)) for s in (1, 2, 3)
    ]
    for copy in sel_out:
        copy.start()
    f = flag[0:1, :]
    fb = f.astype(BF)
    nb = (1.0 - f).astype(BF)

    key = lax.broadcasted_iota(jnp.int32, (256, TILE), 0)
    row = lax.broadcasted_iota(jnp.int32, (256, TILE), 1)
    gap = row + TILE - key
    band = (gap >= 0) & (gap < HD)
    bias[0] = jnp.where(band, 0.0, FAR_OFF)
    reach = TILE * (1 - at.half)
    bias[1] = jnp.where(band & (key >= reach), 0.0, FAR_OFF)
    close = (row - key >= 0) & (row - key < HD)
    bias[2] = jnp.where(
        ((key < TILE) & close) | ((key >= TILE) & ((key - TILE) // HD == row // HD)), 0.0, FAR_OFF
    )
    kvp[:, 0:TILE, :] = jnp.zeros((6, TILE, TILE), BF)
    g.tick()

    normed = layer_norm(tok[...].astype(F32))[0]
    for copy in sel_out:
        copy.wait()
    sel_core = put(selz.at[pl.ds(2 * (1 - at.c), 2)], selp, es.at[3], er.at[3], at.pair)
    sel_core.start()
    g.ready(0, 0)
    odd = at.z % 2
    extra = ga[at.z, :, :, :, 512:640].reshape(D, TILE).astype(F32).T
    even_f = (1 - odd).astype(F32)
    odd_f = odd.astype(F32)
    gain = extra[0:8] * even_f + extra[HD : HD + 8] * odd_f
    gains[...] = gain
    save(gains, gains_o)
    first[...] = (normed * gain[3:4, :]).astype(BF)
    save(first, first_o)
    sel_core.wait()
    fi = f.astype(jnp.int32)
    for i in range(2):
        mine = selz[2 * at.c + i] * (1 - fi) + selp[i] * fi
        selrow[i] = mine
        column = jnp.concatenate([mine.astype(F32), jnp.zeros((TILE - 16, TILE), F32)], 0).T.astype(jnp.int32)
        for r in range(12):
            selcol[i * 12 + r] = jnp.broadcast_to(column[:, r : r + 1], (TILE, TILE))
    save(selrow, sr_o)

    for s in range(TP):
        g.ready(0, s)
        t = g.slot(s)
        w = ga[t].reshape(D, 640)
        extra_side = (lanes((256, TILE)) // HD) == t % 2
        for r in range(0, ROWS, 256):
            got = nn(first[r : r + 256, :], w)
            mixed[t, r : r + 256, 0:512] = got[:, 0:512].astype(BF)
            last = got[:, 512:640]
            soft = jnp.log(1.0 + jnp.exp(-jnp.abs(last)))
            mixed[t, r : r + 256, 512:640] = jnp.where(extra_side, jnp.minimum(last, 0.0) - soft, last).astype(BF)
            sg[t, r : r + 256, :] = (1.0 / (1.0 + jnp.exp(last))).astype(BF)
    save(sg, sg_o)
    save(ga, ga_o)
    swap = [
        put(mixed.at[2 * (1 - at.c) + i], mrecv.at[i], es.at[4 + i], er.at[4 + i], at.pair) for i in range(2)
    ]
    for copy in swap:
        copy.start()
    g.tick()
    for copy in swap:
        copy.wait()
    base = pl.multiple_of(TILE + ROWS * at.half, TILE)
    for i in range(2):
        for j in range(3):
            a = mixed[2 * at.c + i, :, 128 * j : 128 * j + 128]
            b = mrecv[i, :, 128 * j : 128 * j + 128]
            kvp[3 * i + j, pl.ds(base, ROWS), :] = a * fb + b * nb
            kvc[3 * i + j] = a * nb + b * fb
    left = halves((ROWS, TILE))

    def joined(src, index, lo, hi):
        return jnp.where(left, src[index(0), :, lo : lo + 128].astype(F32), src[index(1), :, hi : hi + 128].astype(F32))

    mine = lambda i: 2 * at.c + i
    theirs = lambda i: i
    gate_a = joined(mixed, mine, 512, 512).astype(BF)
    gate_b = joined(mrecv, theirs, 512, 512).astype(BF)
    wanted = (lanes((ROWS, TILE)) % HD) < 3
    gp[pl.ds(pl.multiple_of(ROWS * at.half, ROWS), ROWS), :] = jnp.where(
        wanted, (gate_a * fb + gate_b * nb).astype(F32), 0.0
    ).astype(BF)
    for n in range(3):
        if n == 1:
            a = jnp.where(left, mixed[2 * at.c + 1, :, 512:640].astype(F32), mixed[2 * at.c, :, 512:640].astype(F32)).astype(BF)
            b = jnp.where(left, mrecv[1, :, 512:640].astype(F32), mrecv[0, :, 512:640].astype(F32)).astype(BF)
        else:
            a = mixed[2 * at.c + n // 2, :, 384:512]
            b = mrecv[n // 2, :, 384:512]
        eighth = jnp.asarray(0.125, BF)
        qp[n] = (a * fb + b * nb) * eighth
        qc[n] = (a * nb + b * fb) * eighth

    part = gp.at[pl.ds(pl.multiple_of(ROWS * at.half, ROWS), ROWS)]
    over = [put(part, part, es.at[6], er.at[6], at.zp)]
    for h in range(6):
        part = kvp.at[h, pl.ds(base, ROWS)]
        over.append(put(part, part, es.at[7 + h], er.at[7 + h], at.zp))
    for copy in over:
        copy.start()
    save(qp, qp_o)
    save(qc, qc_o)
    save(kvc, kvc_o)
    g.tick()

    def soft(scores, table):
        scores = scores + table
        top = jnp.max(scores, axis=0, keepdims=True)
        raised = jnp.exp(scores - top)
        return (raised * (1.0 / jnp.sum(raised, axis=0, keepdims=True))).astype(BF)

    def put_shares(h, tile, shares):
        pt[tile // 2, pl.ds(pl.multiple_of(tile % 2 * 256, 256), 256), 128 * h : 128 * h + 128] = shares

    def prompt_tile(n, tau, table):
        start = pl.multiple_of(ROWS * at.half + TILE * tau, TILE)
        rows = pl.ds(pl.multiple_of(TILE * tau, TILE), TILE)
        q = qp[n, rows, :]
        got = []
        for par in range(2):
            kv = kvp[2 * n + par, pl.ds(start, 256), :]
            shares = soft(nt(kv, only(q, par == 1)), table)
            put_shares(2 * n + par, tau, shares)
            got.append(tn(shares, kv))
        atp[n, rows, :] = jnp.where(halves((TILE, TILE)), got[0], got[1]).astype(BF)

    for n in range(3):
        @pl.loop(1, 4)
        def _(tau, n=n):
            prompt_tile(n, tau, bias[0])
        g.tick()

    def pick(h):
        for tau in range(4):
            col = selcol[(h // 3) * 12 + (h % 3) * 4 + tau]
            for b in range(8):
                oh[TILE * tau : TILE * tau + TILE, 128 * b : 128 * b + 128] = jnp.where(
                    col == lanes((TILE, TILE)) + 128 * b, 1.0, 0.0
                ).astype(BF)
        table = jnp.concatenate([kvp[h, TILE : TILE + UNIT, :], gp[...]], 1)
        for r in range(0, ROWS, 256):
            sb[h, r : r + 256, :] = nn(oh[r : r + 256, :], table).astype(BF)

    for copy in over[:1]:
        copy.wait()
    for n in range(3):
        for par in range(2):
            over[1 + 2 * n + par].wait()
        prompt_tile(n, 0, bias[1])
        for par in range(2):
            pick(2 * n + par)

        @pl.loop(0, 4)
        def _(tau, n=n):
            rows = pl.ds(pl.multiple_of(TILE * tau, TILE), TILE)
            q = qc[n, rows, :]
            got = []
            for par in range(2):
                h = 2 * n + par
                far = sb[h, rows, :]
                kv = jnp.concatenate([kvc[h, rows, :], far[:, 0:TILE]], 0)
                gate = jnp.concatenate([jnp.zeros((TILE, TILE), BF), far[:, TILE : 2 * TILE]], 0)
                hot = jnp.where(lanes((TILE, TILE)) == gate_lane(h), 1.0, 0.0).astype(BF)
                scores = nt(jnp.concatenate([kv, gate], 1), jnp.concatenate([only(q, par == 1), hot], 1))
                shares = soft(scores, bias[2])
                put_shares(h, 4 + tau, shares)
                got.append(tn(shares, kv))
            atc[n, rows, :] = jnp.where(halves((TILE, TILE)), got[0], got[1]).astype(BF)
        g.tick()
    save(kvp, kvp_o)
    save(sb, sb_o)
    save(pt, pt_o)

    for n in range(3):
        a, b = atp[n], atc[n]
        att[at.c, n] = a * fb + b * nb
        atp[n] = a * nb + b * fb
    back = put(atp, att.at[at.c], es.at[13], er.at[13], at.pair)
    back.start()
    g.ready(1, 3)
    gwt[...] = jnp.concatenate([gb[t].reshape(D, 256)[:, 0:192] for t in range(TP)], 1)
    save(gwt, gw_o)
    back.wait()
    save(att, att_o)
    for r in range(0, ROWS, 128):
        branch = nt(
            jnp.concatenate([att[k, n, r : r + 128, :] for k in range(2) for n in range(3)], 1), gwt[...]
        )
        kept = tok[r : r + 128, :].astype(F32) + branch
        resid[r : r + 128, :] = kept
        second[r : r + 128, :] = (layer_norm(kept)[0] * gains[4:5, :]).astype(BF)
    save(resid, resid_o)
    for s in range(TP):
        g.ready(2, s)
        t = g.slot(s)
        w = gc[t].reshape(D, 768)
        for r in range(0, ROWS, 128):
            v = nn(second[r : r + 128, :], w)
            square = v * v
            th = jnp.tanh(GELU * (v + CUBE * v * square))
            half = 0.5 * (1.0 + th)
            hid[t, r : r + 128, :] = (v * half).astype(BF)
            slope = half + 0.5 * v * (1.0 - th * th) * (GELU * (1.0 + 3.0 * CUBE * square))
            dg[t, r : r + 128, :] = slope.astype(BF)
    save(hid, hid_o)
    save(dg, dg_o)
    save(gc, gc_o)
    for s in range(TP):
        g.ready(3, s)
        t = g.slot(s)
        w = gd[t].reshape(D, 768)
        for r in range(0, ROWS, 256):
            if s == 0:
                out[r : r + 256, :] = resid[r : r + 256, :] + nt(hid[t, r : r + 256, :], w)
            else:
                out[r : r + 256, :] += nt(hid[t, r : r + 256, :], w)
    save(gd, gd_o)
    g.drain()
    for copy in saved:
        copy.wait()


def forward(tok, pack, sel, flag, inner):
    dma = pltpu.SemaphoreType.DMA
    G = [(TP, 4, 2, 96, c) for c in COLS]
    shapes = [
        ((ROWS, D), F32),
        ((ROWS, D), F32),
        ((8, D), F32),
        ((TP, ROWS, 768), BF),
        ((TP, ROWS, 768), BF),
        ((2, 3, ROWS, TILE), BF),
        ((TP, ROWS, 768), BF),
        ((6, TILE + UNIT, TILE), BF),
        ((6, ROWS, TILE), BF),
        ((3, ROWS, TILE), BF),
        ((3, ROWS, TILE), BF),
        ((6, ROWS, 2 * TILE), BF),
        ((2, 16, TILE), jnp.int32),
        ((TP, ROWS, TILE), BF),
        ((ROWS, D), BF),
        (G[0], BF), ((D, D), BF), (G[2], BF), (G[3], BF),
    ]
    vm = pl.BlockSpec(memory_space=pltpu.VMEM)
    anyw = pl.BlockSpec(memory_space=pl.ANY)
    V = pltpu.VMEM
    scratch = [V(s, BF) for s in G] + [
        V((ROWS, D), BF), V((TP, ROWS, 640), BF), V((2, ROWS, 640), BF), V((TP, ROWS, TILE), BF),
        V((TP, 16, TILE), jnp.int32), V((2, 16, TILE), jnp.int32), V((2, 16, TILE), jnp.int32), V((24, TILE, TILE), jnp.int32),
        V((6, TILE + UNIT, TILE), BF), V((6, ROWS, TILE), BF), V((3, ROWS, TILE), BF), V((3, ROWS, TILE), BF), V((UNIT, TILE), BF),
        V((6, ROWS, 2 * TILE), BF), V((ROWS, UNIT), BF), V((3, 256, TILE), F32), V((TP, ROWS, 768), BF),
        V((3, ROWS, TILE), BF), V((3, ROWS, TILE), BF),
        V((2, 3, ROWS, TILE), BF), V((ROWS, D), F32), V((ROWS, D), BF), V((TP, ROWS, 768), BF), V((TP, ROWS, 768), BF), V((D, D), BF), V((8, D), F32),
        dma((4, 3)), dma((4, 3)), dma((4, 4, 5)), dma((4, 4, 5)), dma((14,)), dma((14,)), dma((18,)),
    ]
    return pl.pallas_call(
        functools.partial(forward_kernel, inner),
        out_shape=[jax.ShapeDtypeStruct(s, d) for s, d in shapes],
        in_specs=[vm] * 4,
        out_specs=[vm] + [anyw] * (len(shapes) - 1),
        scratch_shapes=scratch,
        compiler_params=pltpu.CompilerParams(collective_id=0, has_side_effects=True, vmem_limit_bytes=60 << 20),
    )(tok, pack, sel, flag)


def packed(w_qkv, w_score, w_out, w_fc, w_proj, ln1_gain, ln2_gain):
    odd = lax.axis_index("tp") % 2 == 1
    n = w_qkv.shape[0]
    part = [[w_qkv[:, 192 * j + 64 * m : 192 * j + 64 * m + 64] for m in range(3)] for j in range(3)]
    extra = jnp.concatenate([w_score, ln1_gain[:, None], ln2_gain[:, None], jnp.zeros((n, 59), BF)], 1)
    (q0, k0, v0), (q1, k1, v1), (q2, k2, v2) = part
    even_cols = [v0, k0, k1, v1, v2, k2, q1, q0, extra, q2]
    odd_cols = [k0, v0, v1, k1, k2, v2, q2, q1, q0, extra]
    first = jnp.where(odd, jnp.concatenate(odd_cols, 1), jnp.concatenate(even_cols, 1))
    return jnp.concatenate([first, w_out.T, jnp.zeros((n, 64), BF), w_fc, w_proj.T], 1)


def spread_selected(selected):
    s = selected.reshape(4, 4, 2, 3, 64).transpose(0, 3, 1, 2, 4).reshape(4, 12, 128)
    return jnp.pad(s, ((0, 0), (0, 4), (0, 0)))


def prompt_flag(holder):
    dp = lax.axis_index("dp")
    group = dp // 2 * 2 + lax.axis_index("tp") // 2
    holds = lax.dynamic_index_in_dim(holder, group, 0, False) == dp % 2
    return jnp.broadcast_to(holds.astype(F32), (8, 128))


def start(tokens, w_qkv, w_score, w_out, w_fc, w_proj, ln1_gain, ln2_gain, selected, holder):
    inner = lax.axis_size("dp") // 8
    pack = packed(w_qkv, w_score, w_out, w_fc, w_proj, ln1_gain, ln2_gain)
    if inner > 1:
        groups = [[o * inner + i for i in range(inner)] for o in range(8)]
        pack = lax.all_gather(pack, "dp", axis=0, tiled=True, axis_index_groups=groups)
    flag = prompt_flag(holder)
    return forward(tokens, pack, spread_selected(selected), flag, inner), flag, inner


class Reduce:
    def __init__(self, at, produce, result, refs):
        self.at, self.produce, self.result = at, produce, result
        self.w, self.rc, self.rh, self.rd, self.rz, self.ss, self.rs, self.zs, self.zr = refs
        self.order = [(p, s) for p in (3, 2, 1, 0) for s in (1, 2, 3, 0)]
        self.now = 0

    def slot(self, i):
        return (self.at.z + self.order[i][1]) % TP

    def width(self, i):
        return COLS[self.order[i][0]]

    def copy(self, i, j, src, dst, device):
        return put(src, dst, self.ss.at[i % SLOTS, j], self.rs.at[i % 4, j], device)

    def to_core(self, i):
        c = self.width(i)
        src = self.w.at[i % SLOTS, :, 1 - self.at.cb, :, pl.ds(0, c)]
        return self.copy(i, 0, src, self.rc.at[i % 4, :, :, pl.ds(0, c)], self.at.core)

    def diagonal(self, i, j):
        a, c = self.at, self.width(i)
        src = self.w.at[i % SLOTS, a.d_yx, a.cb, pl.ds(48 * j, 48), pl.ds(0, c)]
        return self.copy(i, 1 + j, src, self.rh.at[i % 4, j, :, pl.ds(0, c)], (a.xn, a.yn)[j])

    def direct(self, i, j):
        a, c = self.at, self.width(i)
        src = self.w.at[i % SLOTS, (a.x_yx, a.y_yx)[j], a.cb, :, pl.ds(0, c)]
        return self.copy(i, 3 + j, src, self.rd.at[i % 4, j, :, pl.ds(0, c)], (a.xn, a.yn)[j])

    def along_z(self, i):
        a, (p, s) = self.at, self.order[i]
        src = self.w.at[i % SLOTS, a.yx, a.cb, :, pl.ds(0, COLS[p])]
        return put(src, self.rz[p].at[s - 1], self.zs.at[p, s - 1], self.zr.at[p, s - 1], a.zdev(s))

    def finish_sends(self, i):
        self.to_core(i).wait_send()
        for j in (0, 1):
            self.diagonal(i, j).wait_send()
            self.direct(i, j).wait_send()
        if self.order[i][1]:
            self.along_z(i).wait_send()

    def tick(self):
        i, n, a, w = self.now, len(self.order), self.at, self.w
        self.now += 1
        if i < n:
            if i >= SLOTS:
                self.finish_sends(i - SLOTS)
            self.produce(i, *self.order[i], self.slot(i))
            self.to_core(i).start()
        if 0 <= i - 1 < n:
            k = i - 1
            c = self.width(k)
            self.to_core(k).wait_recv()
            for q in (a.d_yx, a.x_yx, a.y_yx, a.yx):
                w[k % SLOTS, q, a.cb, :, 0:c] = (
                    w[k % SLOTS, q, a.cb, :, 0:c].astype(F32) + self.rc[k % 4, q, :, 0:c].astype(F32)
                ).astype(BF)
            for j in (0, 1):
                self.diagonal(k, j).start()
        if 0 <= i - 2 < n:
            k = i - 2
            c = self.width(k)
            for j in (0, 1):
                self.diagonal(k, j).wait_recv()
                q, rows = (a.y_yx, a.x_yx)[j], pl.ds(48 * j, 48)
                w[k % SLOTS, q, a.cb, rows, 0:c] = (
                    w[k % SLOTS, q, a.cb, rows, 0:c].astype(F32) + self.rh[k % 4, j, :, 0:c].astype(F32)
                ).astype(BF)
                self.direct(k, 1 - j).start()
        if 0 <= i - 3 < n:
            k = i - 3
            p, s = self.order[k]
            c = COLS[p]
            for j in (0, 1):
                self.direct(k, j).wait_recv()
            total = (
                w[k % SLOTS, a.yx, a.cb, :, 0:c].astype(F32)
                + self.rd[k % 4, 0, :, 0:c].astype(F32)
                + self.rd[k % 4, 1, :, 0:c].astype(F32)
            )
            if s:
                w[k % SLOTS, a.yx, a.cb, :, 0:c] = total.astype(BF)
                self.along_z(k).start()
            else:
                self.result[:, OFF[p] : OFF[p] + c] = total

    def finish(self):
        n = len(self.order)
        while self.now < n + 3:
            self.tick()
        for i in range(n - SLOTS, n):
            self.finish_sends(i)
        for p in (3, 2, 1, 0):
            for s in (1, 2, 3):
                k = self.order.index((p, s))
                self.along_z(k).wait_recv()
            lo, c = OFF[p], COLS[p]
            self.result[:, lo : lo + c] += (
                self.rz[p][0].astype(F32) + self.rz[p][1].astype(F32) + self.rz[p][2].astype(F32)
            )


def norm_back(grad, normed, inverse, gain):
    inner = grad * gain
    return inverse * (
        inner - jnp.mean(inner, -1, keepdims=True) - normed * jnp.mean(inner * normed, -1, keepdims=True)
    )


def backward_kernel(
    inner, tok, cot, flag, gains, selrow, resid_h, first_h, hid_h, dg_h, att_h, pt_h, kvp_h, kvc_h, qp_h, qc_h, sb_h, sg_h,
    ga_h, gw_h, gc_h, gd_h,
    grad_in, grads,
    buf1, buf2, gwt, hid, dg, resid, first, att, kvp, kvc, qp, qc, sb, sg, xt0, xt1, gb, gatt, gattr, acc, gacc, dsel, ot,
    own, away, come, gaway, gcome, gown, dkvc, dqp, dqc, gm, gs, cols, w, rc, rh, rd, rz0, rz1, rz2, rz3,
    ss, rs, zs, zr, es, er, ls,
):
    at = Place(inner)
    loads = {}

    def load(name, src, dst):
        loads[name] = pltpu.make_async_copy(src, dst, ls.at[len(loads)])
        loads[name].start()

    load("hid", hid_h, hid)
    load("gd", gd_h, buf1)
    load("dg", dg_h, dg)
    load("gc", gc_h, buf2)
    load("resid", resid_h, resid)
    load("gw", gw_h, gwt)
    for name, src, dst in (
        ("att", att_h, att), ("kvp", kvp_h, kvp), ("kvc", kvc_h, kvc), ("qp", qp_h, qp), ("qc", qc_h, qc),
        ("sb", sb_h, sb), ("sg", sg_h, sg), ("first", first_h, first),
    ):
        load(name, src, dst)
    f = flag[0:1, :]
    fb = f.astype(BF)
    nb = (1.0 - f).astype(BF)
    at.barrier()

    def flipped(dst, src):
        for r in range(0, ROWS, 128):
            for q in range(0, D, 128):
                dst[q : q + 128, r : r + 128] = src[r : r + 128, q : q + 128].astype(F32).T.astype(BF)

    def produce(i, p, s, t):
        left = (xt1, xt0, xt1, xt0)[p]
        if p == 3:
            right = hid[t]
        elif p == 2:
            right = dg[t]
        elif p == 0:
            right = gm[t]
        c = COLS[p]
        if p == 1:
            whole = jnp.concatenate([att[k, n] for k in range(2) for n in range(3)], 1)
            right = jnp.concatenate([whole[:, 0:192], jnp.zeros((ROWS, 64), BF)], 1)
            for o in range(1, 4):
                cut = jnp.concatenate([whole[:, 192 * o : 192 * o + 192], jnp.zeros((ROWS, 64), BF)], 1)
                right = jnp.where(t == o, cut, right)
        for k in range(8):
            block = nn(left[96 * k : 96 * k + 96, :], right)
            if p == 0:
                w[i % SLOTS, k // 2, k % 2, :, 0:512] = block[:, 0:512].astype(BF)
                side = (lanes((96, TILE)) // HD) == t % 2
                w[i % SLOTS, k // 2, k % 2, :, 512:640] = (
                    block[:, 512:640] + jnp.where(side, cols[96 * k : 96 * k + 96, :], 0.0)
                ).astype(BF)
            else:
                w[i % SLOTS, k // 2, k % 2, :, 0:c] = block.astype(BF)

    red = Reduce(at, produce, grads, (w, rc, rh, rd, (rz0, rz1, rz2, rz3), ss, rs, zs, zr))

    flipped(xt0, cot)
    loads["hid"].wait()
    loads["gd"].wait()
    loads["dg"].wait()
    for s in (1, 2, 3, 0):
        red.tick()
        t = (at.z + s) % TP
        weight = buf1[t].reshape(D, 768)
        for r in range(0, ROWS, 128):
            got = nn(cot[r : r + 128, :], weight)
            dg[t, r : r + 128, :] = (got * dg[t, r : r + 128, :].astype(F32)).astype(BF)
    load("pt", pt_h, hid)
    load("ga", ga_h, buf1.at[:, :, :, :, pl.ds(0, 640)])
    loads["gc"].wait()
    loads["resid"].wait()
    loads["gw"].wait()
    gain_one, gain_two = gains[3:4, :], gains[4:5, :]
    part_two = jnp.zeros((1, D), F32)
    for r in range(0, ROWS, 128):
        got = nt(dg[0, r : r + 128, :], buf2[0].reshape(D, 768))
        for t in range(1, TP):
            got += nt(dg[t, r : r + 128, :], buf2[t].reshape(D, 768))
        normed, inverse = layer_norm(resid[r : r + 128, :])
        part_two += jnp.sum(got * normed, 0, keepdims=True)
        back = cot[r : r + 128, :].astype(F32) + norm_back(got, normed, inverse, gain_two)
        grad_in[r : r + 128, :] = back
        gb[r : r + 128, :] = back.astype(BF)
        xt1_rows = (normed * gain_two).astype(BF).astype(F32)
        for q in range(0, D, 128):
            xt1[q : q + 128, r : r + 128] = xt1_rows[:, q : q + 128].T.astype(BF)
        grad_att = nn(back.astype(BF), gwt[...]).astype(BF)
        for k in range(2):
            for n in range(3):
                gatt[k, n, r : r + 128, :] = grad_att[:, 384 * k + 128 * n : 384 * k + 128 * n + 128]
    swap = put(gatt.at[1 - at.c], gattr, es.at[0], er.at[0], at.pair)
    swap.start()
    flipped(xt0, gb)
    red.tick()
    for name in ("att", "kvp", "kvc", "qp", "qc", "sb", "sg", "first", "pt", "ga"):
        loads[name].wait()
    swap.wait()
    for n in range(3):
        a, b = gatt[at.c, n], gattr[n]
        gatt[at.c, n] = a * fb + b * nb
        gattr[n] = a * nb + b * fb

    gacc[...] = jnp.zeros_like(gacc)
    low_lanes = halves((TILE, TILE))
    mine = pl.multiple_of(TILE + ROWS * at.half, TILE)
    other = pl.multiple_of(TILE + ROWS * (1 - at.half), TILE)
    over = []

    def shares_of(h, tile):
        return hid[tile // 2, pl.ds(pl.multiple_of(tile % 2 * 256, 256), 256), 128 * h : 128 * h + 128]

    def slope(shares, kv, up):
        spread = nt(kv, up)
        p = shares.astype(F32)
        prod = p * spread
        return (prod - p * jnp.sum(prod, 0, keepdims=True)).astype(BF)

    for n in range(3):
        @pl.loop(0, 4)
        def _(tau, n=n):
            rows = pl.ds(pl.multiple_of(TILE * tau, TILE), TILE)
            q = qc[n, rows, :]
            up_pair = gattr[n, rows, :]
            got = []
            for par in range(2):
                h = 2 * n + par
                far = sb[h, rows, :]
                kv = jnp.concatenate([kvc[h, rows, :], far[:, 0:TILE]], 0)
                hot = jnp.where(lanes((TILE, TILE)) == gate_lane(h), 1.0, 0.0).astype(BF)
                up = only(up_pair, par == 0)
                shares = shares_of(h, 4 + tau)
                down = slope(shares, kv, up)
                grad = nn(
                    jnp.concatenate([down, shares], 1),
                    jnp.concatenate(
                        [jnp.concatenate([only(q, par == 1), hot], 1), jnp.concatenate([up, jnp.zeros_like(up)], 1)], 0
                    ),
                )
                dkvc[h, rows, :] = grad[0:TILE, 0:TILE].astype(BF)
                dsel[par, rows, :] = grad[TILE:256, :].astype(BF)
                got.append(tn(down, kv))
            dqc[n, rows, :] = (jnp.where(low_lanes, got[1], got[0]) * 0.125).astype(BF)

        red.tick()
        for par in range(2):
            h = 2 * n + par
            for tau in range(4):
                row = (h % 3) * 4 + tau
                pick = jnp.broadcast_to(selrow[h // 3, row : row + 1, :], (TILE, TILE))
                for b in range(8):
                    ot[128 * b : 128 * b + 128, 128 * tau : 128 * tau + 128] = jnp.where(
                        pick == lax.broadcasted_iota(jnp.int32, (TILE, TILE), 0) + 128 * b, 1.0, 0.0
                    ).astype(BF)
            acc[par, 0:TILE, :] = jnp.zeros((TILE, TILE), F32)
            for r in range(0, UNIT, 256):
                got = nn(ot[r : r + 256, :], dsel[par])
                acc[par, TILE + r : TILE + r + 256, :] = got[:, 0:TILE]
                gacc[r : r + 256, :] += got[:, TILE : 2 * TILE]

        @pl.loop(0, 4)
        def _(tau, n=n):
            start = pl.multiple_of(ROWS * at.half + TILE * tau, TILE)
            rows = pl.ds(pl.multiple_of(TILE * tau, TILE), TILE)
            q = qp[n, rows, :]
            up_pair = gatt[at.c, n, rows, :]
            got = []
            for par in range(2):
                h = 2 * n + par
                kv = kvp[h, pl.ds(start, 256), :]
                up = only(up_pair, par == 0)
                shares = shares_of(h, tau)
                down = slope(shares, kv, up)
                acc[par, pl.ds(start, 256), :] += nn(
                    jnp.concatenate([down, shares], 1), jnp.concatenate([only(q, par == 1), up], 0)
                )
                got.append(tn(down, kv))
            dqp[n, rows, :] = (jnp.where(low_lanes, got[1], got[0]) * 0.125).astype(BF)

        for par in range(2):
            h = 2 * n + par
            away[h] = acc[par, pl.ds(other, ROWS), :].astype(BF)
            own[h] = acc[par, pl.ds(mine, ROWS), :].astype(BF)
            over.append(put(away.at[h], come.at[h], es.at[1 + h], er.at[1 + h], at.zp))
            over[-1].start()
        red.tick()
    gaway[...] = gacc[pl.ds(pl.multiple_of(ROWS * (1 - at.half), ROWS), ROWS), :].astype(BF)
    over.append(put(gaway, gcome, es.at[7], er.at[7], at.zp))
    over[-1].start()
    red.tick()
    for copy in over:
        copy.wait()
    gate = (gacc[pl.ds(pl.multiple_of(ROWS * at.half, ROWS), ROWS), :] + gcome[...].astype(F32)).astype(BF)

    def deal(i, lo, a, b):
        gm[2 * at.c + i, :, lo : lo + 128] = a * fb + b * nb
        gs[i, :, lo : lo + 128] = a * nb + b * fb

    for h in range(6):
        deal(h // 3, 128 * (h % 3), (own[h].astype(F32) + come[h].astype(F32)).astype(BF), dkvc[h])
    deal(0, 384, dqp[0], dqc[0])
    deal(1, 384, dqp[2], dqc[2])
    left = halves((ROWS, TILE))
    middle, zero = dqp[1].astype(F32), jnp.zeros((ROWS, TILE), F32)
    middle_c = dqc[1].astype(F32)
    gate = gate.astype(F32)
    deal(0, 512, jnp.where(left, gate, middle).astype(BF), jnp.where(left, zero, middle_c).astype(BF))
    deal(1, 512, jnp.where(left, middle, gate).astype(BF), jnp.where(left, middle_c, zero).astype(BF))
    swap = [put(gs.at[i], gm.at[2 * at.c + i], es.at[8 + i], er.at[8 + i], at.pair) for i in range(2)]
    for copy in swap:
        copy.start()
    while red.now < 12:
        red.tick()
    flipped(xt1, first)
    for copy in swap:
        copy.wait()
    for t in range(TP):
        side = left if t % 2 == 0 else jnp.logical_not(left)
        last = gm[t, :, 512:640].astype(F32)
        gm[t, :, 512:640] = jnp.where(side, last * sg[t].astype(F32), last).astype(BF)
    part_one = jnp.zeros((1, D), F32)
    for r in range(0, ROWS, 128):
        got = nt(gm[0, r : r + 128, :], buf1[0, :, :, :, 0:640].reshape(D, 640))
        for t in range(1, TP):
            got += nt(gm[t, r : r + 128, :], buf1[t, :, :, :, 0:640].reshape(D, 640))
        normed, inverse = layer_norm(tok[r : r + 128, :].astype(F32))
        part_one += jnp.sum(got * normed, 0, keepdims=True)
        grad_in[r : r + 128, :] += norm_back(got, normed, inverse, gain_one)
    gap = jnp.zeros((3, D), F32)
    block = jnp.concatenate([gap, part_one, part_two, gap], 0)
    wide = jnp.concatenate([block, jnp.zeros((56, D), F32), block, jnp.zeros((56, D), F32)], 0)
    cols[...] = wide.T
    red.finish()


def backward(tok, cot, flag, kept, inner):
    (resid, gains, hid, dg, att, pt, kvp, kvc, qp, qc, sb, selrow, sg, first, ga, gw, gc, gd) = kept
    dma = pltpu.SemaphoreType.DMA
    V = pltpu.VMEM
    vm = pl.BlockSpec(memory_space=pltpu.VMEM)
    anyw = pl.BlockSpec(memory_space=pl.ANY)
    G = (TP, 4, 2, 96, 768)
    wide = V((TP, ROWS, 768), BF)
    sq = V((ROWS, D), BF)
    three = V((3, ROWS, TILE), BF)
    six = V((6, ROWS, TILE), BF)
    scratch = [
        V(G, BF), V(G, BF), V((D, D), BF), wide, wide, V((ROWS, D), F32), sq, V((2, 3, ROWS, TILE), BF),
        V((6, TILE + UNIT, TILE), BF), six, three, three, V((6, ROWS, 2 * TILE), BF), V((TP, ROWS, TILE), BF),
        V((D, ROWS), BF), V((D, ROWS), BF), sq, V((2, 3, ROWS, TILE), BF), three,
        V((2, TILE + UNIT, TILE), F32), V((UNIT, TILE), F32), V((2, ROWS, 2 * TILE), BF), V((UNIT, ROWS), BF),
        six, six, six, V((ROWS, TILE), BF), V((ROWS, TILE), BF), V((ROWS, TILE), BF), six, three, three,
        V((TP, ROWS, 640), BF), V((2, ROWS, 640), BF), V((D, TILE), F32),
        V((SLOTS, 4, 2, 96, 768), BF), V((4, 4, 96, 768), BF), V((4, 2, 48, 768), BF), V((4, 2, 96, 768), BF),
    ] + [V((3, 96, c), BF) for c in COLS] + [
        dma((SLOTS, 5)), dma((4, 5)), dma((4, 3)), dma((4, 3)), dma((10,)), dma((10,)), dma((16,)),
    ]
    return pl.pallas_call(
        functools.partial(backward_kernel, inner),
        out_shape=[jax.ShapeDtypeStruct((ROWS, D), F32), jax.ShapeDtypeStruct((96, WIDE), F32)],
        in_specs=[vm] * 5 + [anyw] * 16,
        out_specs=[vm, vm],
        scratch_shapes=scratch,
        compiler_params=pltpu.CompilerParams(collective_id=1, has_side_effects=True, vmem_limit_bytes=62 << 20),
    )(tok, cot, flag, gains, selrow, resid, first, hid, dg, att, pt, kvp, kvc, qp, qc, sb, sg, ga, gw, gc, gd)


def unpacked(grads):
    odd = lax.axis_index("tp") % 2 == 1
    piece = [grads[:, 64 * k : 64 * k + 64] for k in range(10)]
    even_cols = [7, 1, 0, 6, 2, 3, 9, 5, 4]
    odd_cols = [8, 0, 1, 7, 3, 2, 6, 4, 5]
    qkv = jnp.where(
        odd, jnp.concatenate([piece[k] for k in odd_cols], 1), jnp.concatenate([piece[k] for k in even_cols], 1)
    )
    extra = jnp.where(odd, piece[9], piece[8])[:, 0:5]
    return (
        qkv, extra[:, 0:3], grads[:, 640:832].T, grads[:, 896:1664], grads[:, 1664:2432].T, extra[:, 3], extra[:, 4]
    )


def per_device(
    tokens, w_qkv, w_score, w_out, w_fc, w_proj, ln1_gain, ln2_gain, selected, holder, cotangent
):
    kept, flag, inner = start(tokens, w_qkv, w_score, w_out, w_fc, w_proj, ln1_gain, ln2_gain, selected, holder)
    grad_in, grads = backward(tokens, cotangent, flag, kept[1:], inner)
    if inner > 1:
        groups = [[o * inner + i for i in range(inner)] for o in range(8)]
        grads = lax.psum_scatter(grads, "dp", scatter_dimension=0, tiled=True, axis_index_groups=groups)
    return (kept[0], grad_in) + unpacked(grads)


def solution(mesh):
    rows = P(("dp", "tp"), None)
    cols, flip = P("dp", "tp"), P("tp", "dp")
    return jax.shard_map(
        per_device,
        mesh=mesh,
        in_specs=(rows, cols, cols, flip, cols, flip, P("dp"), P("dp"), P("dp", "tp", None), P(), rows),
        out_specs=(rows, rows, cols, cols, flip, cols, flip, P("dp"), P("dp")),
        check_vma=False,
    )
```

```python
import functools
import math

import jax
import jax.numpy as jnp
from jax import lax
from jax.experimental import pallas as pl
from jax.experimental.pallas import tpu as pltpu
from jax.sharding import PartitionSpec as P

MESH = pl.DeviceIdType.MESH
BF = jnp.bfloat16
F32 = jnp.float32
D = 768
HD = 64
COLS = (640, 256, 768, 768)
OFF = (0, 640, 896, 1664)
WIDE = 2432
ALL = 2560
TP = 4
ROWS = 512
UNIT = 1024
TILE = 128
EPS = 1e-05
FAR_OFF = -1e30
GELU = 0.7978845608
CUBE = 0.044715
SLOTS = 5
EARLY = 10
ZPLAN = (-2, 0, 2, 5)
AHEAD = (1, 1, 1, 1)
LATE = 11


def nn(left, right):
    return jnp.dot(left, right, preferred_element_type=F32)


def nt(left, right):
    return lax.dot_general(left, right, (((1,), (1,)), ((), ())), preferred_element_type=F32)


def tn(left, right):
    return lax.dot_general(left, right, (((0,), (0,)), ((), ())), preferred_element_type=F32)


class Place:
    def __init__(self, inner):
        self.inner = inner
        self.dp = lax.axis_index("dp")
        self.z = lax.axis_index("tp")
        self.k = self.dp // inner
        self.cb = self.k % 2
        self.yx = self.k // 2
        self.core = (self.flip(1), self.z)
        self.xn = (self.flip(2), self.z)
        self.yn = (self.flip(4), self.z)
        self.c = self.dp % 2
        self.pair = (self.dp + 1 - 2 * self.c, self.z)
        self.half = self.z % 2
        self.zp = (self.dp, self.z + 1 - 2 * self.half)
        self.x_yx = self.yx + 1 - 2 * (self.yx % 2)
        self.y_yx = self.yx + 2 - 4 * (self.yx // 2)
        self.d_yx = 3 - self.yx

    def flip(self, bit):
        on = self.k // bit % 2
        return self.dp + (1 - 2 * on) * bit * self.inner

    def zdev(self, s):
        return (self.dp, (self.z + s) % TP)

    def barrier(self):
        devices = [self.core, self.xn, self.yn] + [self.zdev(s) for s in (1, 2, 3)]
        if self.inner > 1:
            devices.append(self.pair)
        sem = pltpu.get_barrier_semaphore()
        for device in devices:
            pl.semaphore_signal(sem, inc=1, device_id=device, device_id_type=MESH)
        pl.semaphore_wait(sem, len(devices))


def put(src, dst, send, recv, device):
    return pltpu.make_async_remote_copy(
        src_ref=src, dst_ref=dst, send_sem=send, recv_sem=recv, device_id=device, device_id_type=MESH
    )


class Gather:
    def __init__(self, at, own, bufs, sems):
        self.at, self.own, self.bufs = at, own, bufs
        self.zs, self.zr, self.ps, self.pr = sems
        self.order = [(p, s) for p in range(4) for s in range(4)]
        self.now = -1

    def slot(self, s):
        return (self.at.z - s + TP) % TP

    def along_z(self, p, s):
        a = self.at
        return put(
            self.own[p], self.bufs[p].at[a.z, a.yx, a.cb], self.zs.at[p, s - 1], self.zr.at[p, s - 1], a.zdev(s)
        )

    def along_xy(self, p, s, j):
        a = self.at
        ref = self.bufs[p].at[self.slot(s), a.yx, a.cb]
        return put(ref, ref, self.ps.at[p, s, j], self.pr.at[p, s, j], (a.xn, a.yn)[j])

    def forward(self, p, s, j):
        a = self.at
        ref = self.bufs[p].at[self.slot(s), (a.x_yx, a.y_yx)[j], a.cb, pl.ds(j * 48, 48)]
        return put(ref, ref, self.ps.at[p, s, 2 + j], self.pr.at[p, s, 2 + j], (a.yn, a.xn)[j])

    def to_core(self, p, s):
        a = self.at
        ref = self.bufs[p].at[self.slot(s), :, a.cb]
        return put(ref, ref, self.ps.at[p, s, 4], self.pr.at[p, s, 4], a.core)

    def start_z(self, p):
        for s in (1, 2, 3):
            self.along_z(p, s).start()

    def tick(self):
        i, n = self.now, len(self.order)
        self.now += 1
        if i in ZPLAN:
            self.start_z(ZPLAN.index(i))
        for k in range(n):
            if max(k - AHEAD[k // 4], -1) == i:
                p, s = self.order[k]
                if s:
                    self.along_z(p, s).wait_recv()
                for j in (0, 1):
                    self.along_xy(p, s, j).start()
        if 0 <= i - 1 < n:
            p, s = self.order[i - 1]
            for j in (0, 1):
                self.along_xy(p, s, j).wait_recv()
                self.forward(p, s, j).start()
        if 0 <= i - 2 < n:
            p, s = self.order[i - 2]
            for j in (0, 1):
                self.forward(p, s, j).wait_recv()
            self.to_core(p, s).start()
        if 0 <= i - 3 < n:
            self.to_core(*self.order[i - 3]).wait_recv()

    def ready(self, p, s):
        while self.now <= self.order.index((p, s)) + 3:
            self.tick()

    def drain(self):
        self.ready(3, 3)
        for p, s in self.order:
            if s:
                self.along_z(p, s).wait_send()
            for j in (0, 1):
                self.along_xy(p, s, j).wait_send()
                self.forward(p, s, j).wait_send()
            self.to_core(p, s).wait_send()


def layer_norm(rows):
    center = rows - jnp.mean(rows, axis=-1, keepdims=True)
    spread = jnp.mean(center * center, axis=-1, keepdims=True)
    inverse = lax.rsqrt(spread + EPS)
    return center * inverse, inverse


def lanes(shape):
    return lax.broadcasted_iota(jnp.int32, shape, len(shape) - 1)


def halves(shape):
    return lanes(shape) < HD


def only(tile, left):
    keep = halves(tile.shape)
    return jnp.where(keep if left else jnp.logical_not(keep), tile.astype(F32), 0.0).astype(tile.dtype)


def gate_lane(head):
    return head if head < 3 else HD + head - 3


class Reduce:
    def __init__(self, at, produce, result, refs):
        self.at, self.produce, self.result = at, produce, result
        self.w, self.rc, self.rh, self.rd, self.rz, self.ss, self.rs, self.zs, self.zr = refs
        self.order = [(p, s) for p in (3, 2, 1, 0) for s in (1, 2, 3, 0)] + [(4, 0)]
        self.wide = COLS + (TILE,)
        self.off = OFF + (WIDE,)
        self.now = 0

    def slot(self, i):
        return (self.at.z + self.order[i][1]) % TP

    def width(self, i):
        return self.wide[self.order[i][0]]

    def copy(self, i, j, src, dst, device):
        return put(src, dst, self.ss.at[i % SLOTS, j], self.rs.at[i % 4, j], device)

    def to_core(self, i):
        c = self.width(i)
        src = self.w.at[i % SLOTS, :, 1 - self.at.cb, :, pl.ds(0, c)]
        return self.copy(i, 0, src, self.rc.at[i % 4, :, :, pl.ds(0, c)], self.at.core)

    def diagonal(self, i, j):
        a, c = self.at, self.width(i)
        src = self.w.at[i % SLOTS, a.d_yx, a.cb, pl.ds(48 * j, 48), pl.ds(0, c)]
        return self.copy(i, 1 + j, src, self.rh.at[i % 4, j, :, pl.ds(0, c)], (a.xn, a.yn)[j])

    def direct(self, i, j):
        a, c = self.at, self.width(i)
        src = self.w.at[i % SLOTS, (a.x_yx, a.y_yx)[j], a.cb, :, pl.ds(0, c)]
        return self.copy(i, 3 + j, src, self.rd.at[i % 4, j, :, pl.ds(0, c)], (a.xn, a.yn)[j])

    def along_z(self, i, far=None):
        a, (p, s) = self.at, self.order[i]
        s = far or s
        src = self.w.at[i % SLOTS, a.yx, a.cb, :, pl.ds(0, self.wide[p])]
        return put(src, self.rz[p].at[s - 1], self.zs.at[p, s - 1], self.zr.at[p, s - 1], a.zdev(s))

    def to_z(self, i):
        p, s = self.order[i]
        return [self.along_z(i, far) for far in ((1, 2, 3) if p == 4 else (s,) if s else ())]

    def finish_sends(self, i):
        self.to_core(i).wait_send()
        for j in (0, 1):
            self.diagonal(i, j).wait_send()
            self.direct(i, j).wait_send()
        for copy in self.to_z(i):
            copy.wait_send()

    def tick(self):
        i, n, a, w = self.now, len(self.order), self.at, self.w
        self.now += 1
        if i < n:
            if i >= SLOTS:
                self.finish_sends(i - SLOTS)
            self.produce(i, *self.order[i], self.slot(i))
            self.to_core(i).start()
        if 0 <= i - 1 < n:
            k = i - 1
            c = self.width(k)
            self.to_core(k).wait_recv()
            for q in (a.d_yx, a.x_yx, a.y_yx, a.yx):
                w[k % SLOTS, q, a.cb, :, 0:c] = (
                    w[k % SLOTS, q, a.cb, :, 0:c].astype(F32) + self.rc[k % 4, q, :, 0:c].astype(F32)
                ).astype(BF)
            for j in (0, 1):
                self.diagonal(k, j).start()
        if 0 <= i - 2 < n:
            k = i - 2
            c = self.width(k)
            for j in (0, 1):
                self.diagonal(k, j).wait_recv()
                q, rows = (a.y_yx, a.x_yx)[j], pl.ds(48 * j, 48)
                w[k % SLOTS, q, a.cb, rows, 0:c] = (
                    w[k % SLOTS, q, a.cb, rows, 0:c].astype(F32) + self.rh[k % 4, j, :, 0:c].astype(F32)
                ).astype(BF)
                self.direct(k, 1 - j).start()
        if 0 <= i - 3 < n:
            k = i - 3
            p, s = self.order[k]
            c = self.wide[p]
            for j in (0, 1):
                self.direct(k, j).wait_recv()
            total = (
                w[k % SLOTS, a.yx, a.cb, :, 0:c].astype(F32)
                + self.rd[k % 4, 0, :, 0:c].astype(F32)
                + self.rd[k % 4, 1, :, 0:c].astype(F32)
            )
            if s or p == 4:
                w[k % SLOTS, a.yx, a.cb, :, 0:c] = total.astype(BF)
                for copy in self.to_z(k):
                    copy.start()
            if not s:
                self.result[:, self.off[p] : self.off[p] + c] = total

    def finish(self):
        n = len(self.order)
        while self.now < n + 3:
            self.tick()
        for i in range(n - SLOTS, n):
            self.finish_sends(i)
        for p in (3, 2, 1, 0, 4):
            for s in (1, 2, 3):
                self.along_z(self.order.index((p, 0 if p == 4 else s)), s).wait_recv()
            lo, c = self.off[p], self.wide[p]
            self.result[:, lo : lo + c] += (
                self.rz[p][0].astype(F32) + self.rz[p][1].astype(F32) + self.rz[p][2].astype(F32)
            )


def norm_back(grad, normed, inverse, gain):
    inner = grad * gain
    return inverse * (
        inner - jnp.mean(inner, -1, keepdims=True) - normed * jnp.mean(inner * normed, -1, keepdims=True)
    )


def layer_kernel(
    inner, tok, cot, w_qkv, w_score, w_out, w_fc, w_proj, gain_rows, sel, holder,
    out_h, gin_h, grads, pt_h,
    ga, gb, gc, gd, pack, first, mixed, mrecv, sg, selz, selp, selq, selrow, kvp, kvc, qp, qc, gp, sb, oh, bias, atpc,
    att, resid, second, hid, dg, gwt, gains, wide, xt0, xt1, gattr, acc, gacc, dsel, come, gaway, gcome, cols,
    w, rc, rh, rd, rz0, rz1, rz2, rz3, rz4,
    zs, zr, ps, pr, es, er, ls, ss, rs, rzs, rzr,
):
    at = Place(inner)
    bufs = (ga, gb, gc, gd)
    own = [pack.at[:, pl.ds(OFF[p], COLS[p])] for p in range(4)]
    g = Gather(at, own, bufs, (zs, zr, ps, pr))
    atp, atc, gm, gs = atpc.at[0], atpc.at[1], mixed, mrecv
    odd = at.z % 2
    tiles = [slice(128 * k, 128 * k + 128) for k in range(6)]

    def flipped(dst, src):
        for r in range(0, ROWS, 128):
            for cut in tiles:
                dst[cut, r : r + 128] = src[r : r + 128, cut].astype(F32).T.astype(BF)

    is_odd = lanes((96, TILE)) * 0 + odd == 1
    q0, k0, v0, q1, k1, v1, q2, k2, v2 = [w_qkv[:, 64 * k : 64 * k + 64].astype(F32) for k in range(9)]
    rowed = jnp.concatenate([gain_rows[...].astype(F32), jnp.zeros((2, 32), F32)], 1)
    gain_cols = jnp.concatenate([rowed, jnp.zeros((TILE - 2, TILE), F32)], 0).T[0:96, :]
    small = lanes((96, HD))
    extra = jnp.zeros((96, HD), F32)
    for j in range(3):
        extra = jnp.where(small == j, w_score[:, j : j + 1].astype(F32), extra)
    for j in range(2):
        extra = jnp.where(small == 3 + j, gain_cols[:, j : j + 1], extra)
    even_cols = ((v0, k0), (k1, v1), (v2, k2), (q1, q0), (extra, q2))
    odd_cols = ((k0, v0), (v1, k1), (k2, v2), (q2, q1), (q0, extra))
    for k in range(5):
        tile = jnp.where(is_odd, jnp.concatenate(odd_cols[k], 1), jnp.concatenate(even_cols[k], 1)).astype(BF)
        pack[:, tiles[k]] = tile
        ga[at.z, at.yx, at.cb, :, tiles[k]] = tile
    at.barrier()
    g.start_z(0)
    g.tick()

    def blocks_of(z):
        return pl.ds(pl.multiple_of(8 * z, 8), 8)

    selz[at.z] = sel[blocks_of(at.z)]
    sel_out = [
        put(sel.at[blocks_of((at.z + s) % TP)], selz.at[at.z], es.at[s - 1], er.at[s - 1], at.zdev(s)) for s in (1, 2, 3)
    ]
    for copy in sel_out:
        copy.start()
    flipped_out = jnp.concatenate([w_out[...].astype(F32), jnp.zeros((64, 96), F32)], 0)
    pack[:, 640:896] = flipped_out.T.astype(BF)
    pack[:, 896:1664] = w_fc[...]
    pack[:, 1664:2432] = w_proj[...].astype(F32).T.astype(BF)
    for p in (1, 2, 3):
        bufs[p][at.z, at.yx, at.cb] = own[p][...]
    g.tick()
    f = jnp.full((1, TILE), jnp.where(holder[at.dp // 2 * 2 + at.z // 2] == at.c, 1.0, 0.0), F32)
    fb = f.astype(BF)
    nb = (1.0 - f).astype(BF)

    key = lax.broadcasted_iota(jnp.int32, (256, TILE), 0)
    row = lax.broadcasted_iota(jnp.int32, (256, TILE), 1)
    gap = row + TILE - key
    band = (gap >= 0) & (gap < HD)
    bias[0] = jnp.where(band, 0.0, FAR_OFF)
    reach = TILE * (1 - at.half)
    bias[1] = jnp.where(band & (key >= reach), 0.0, FAR_OFF)
    close = (row - key >= 0) & (row - key < HD)
    bias[2] = jnp.where(
        ((key < TILE) & close) | ((key >= TILE) & ((key - TILE) // HD == row // HD)), 0.0, FAR_OFF
    )
    kvp[:, 0:TILE, :] = jnp.zeros((6, TILE, TILE), BF)

    normed = layer_norm(tok[...].astype(F32))[0]
    for copy in sel_out:
        copy.wait()
    sel_core = put(selz.at[pl.ds(2 * (1 - at.c), 2)], selp, es.at[3], er.at[3], at.pair)
    sel_core.start()
    flipped(xt0, cot)
    g.ready(0, 0)
    extra = ga[at.z, :, :, :, 512:640].reshape(D, TILE).astype(F32).T
    odd_f = odd.astype(F32)
    gains[...] = extra[0:8] * (1.0 - odd_f) + extra[HD : HD + 8] * odd_f
    gain_one, gain_two = gains[3:4, :], gains[4:5, :]
    first[...] = (normed * gain_one).astype(BF)
    sel_core.wait()
    fi = f.astype(jnp.int32)[:, 0:64]
    columns = []
    for i in range(2):
        for k in range(8):
            chosen = selz[2 * at.c + i, k] * (1 - fi) + selp[i, k] * fi
            for j in range(3):
                selq[i, 8 * j + k : 8 * j + k + 1, :] = chosen[j : j + 1, :]
        both = selq[i]
        square = jnp.concatenate([both.astype(F32), jnp.zeros((104, HD), F32)], 0)
        columns.append(jnp.concatenate([square, jnp.zeros((TILE, HD), F32)], 1).T.astype(jnp.int32))
        for r in range(12):
            selrow[i, r : r + 1, :] = jnp.concatenate([both[2 * r : 2 * r + 1, :], both[2 * r + 1 : 2 * r + 2, :]], 1)

    for s in range(TP):
        g.ready(0, s)
        t = g.slot(s)
        weight = ga[t].reshape(D, 640)
        extra_side = (lanes((256, TILE)) // HD) == t % 2
        for r in range(0, ROWS, 256):
            got = nn(first[r : r + 256, :], weight)
            mixed[t, r : r + 256, 0:512] = got[:, 0:512].astype(BF)
            last = got[:, 512:640]
            soft_part = jnp.log(1.0 + jnp.exp(-jnp.abs(last)))
            mixed[t, r : r + 256, 512:640] = jnp.where(
                extra_side, jnp.minimum(last, 0.0) - soft_part, last
            ).astype(BF)
            sg[t, r : r + 256, :] = (1.0 / (1.0 + jnp.exp(last))).astype(BF)
    swap = [
        put(mixed.at[2 * (1 - at.c) + i], mrecv.at[i], es.at[4 + i], er.at[4 + i], at.pair) for i in range(2)
    ]
    for copy in swap:
        copy.start()
    g.tick()
    for copy in swap:
        copy.wait()
    base = pl.multiple_of(TILE + ROWS * at.half, TILE)
    other = pl.multiple_of(TILE + ROWS * (1 - at.half), TILE)
    gate_base = pl.multiple_of(ROWS * at.half, ROWS)
    left = halves((ROWS, TILE))
    gate_own = jnp.where(left, mixed[2 * at.c, :, 512:640].astype(F32), mixed[2 * at.c + 1, :, 512:640].astype(F32))
    gate_pair = jnp.where(left, mrecv[0, :, 512:640].astype(F32), mrecv[1, :, 512:640].astype(F32))
    wanted = (lanes((ROWS, TILE)) % HD) < 3
    gp[pl.ds(gate_base, ROWS), :] = jnp.where(wanted, gate_own * f + gate_pair * (1.0 - f), 0.0).astype(BF)
    part = gp.at[pl.ds(gate_base, ROWS)]
    over = [put(part, part, es.at[6], er.at[6], at.zp)]
    over[0].start()
    for i in range(2):
        for j in range(3):
            a = mixed[2 * at.c + i, :, tiles[j]]
            b = mrecv[i, :, tiles[j]]
            h = 3 * i + j
            kvp[h, pl.ds(base, ROWS), :] = a * fb + b * nb
            part = kvp.at[h, pl.ds(base, ROWS)]
            over.append(put(part, part, es.at[7 + h], er.at[7 + h], at.zp))
            over[-1].start()
            kvc[h] = a * nb + b * fb
    for n in range(3):
        if n == 1:
            a = jnp.where(left, mixed[2 * at.c + 1, :, 512:640].astype(F32), mixed[2 * at.c, :, 512:640].astype(F32)).astype(BF)
            b = jnp.where(left, mrecv[1, :, 512:640].astype(F32), mrecv[0, :, 512:640].astype(F32)).astype(BF)
        else:
            a = mixed[2 * at.c + n // 2, :, 384:512]
            b = mrecv[n // 2, :, 384:512]
        eighth = jnp.asarray(0.125, BF)
        qp[n] = (a * fb + b * nb) * eighth
        qc[n] = (a * nb + b * fb) * eighth
    g.tick()

    low_lanes = halves((TILE, TILE))

    def soft(scores, table):
        scores = scores + table
        top = jnp.max(scores, axis=0, keepdims=True)
        raised = jnp.exp(scores - top)
        return (raised * (1.0 / jnp.sum(raised, axis=0, keepdims=True))).astype(BF)

    def shares_at(h, tile):
        return tile // 2, slice(tile % 2 * 256, tile % 2 * 256 + 256), tiles[h]

    def near_keys(h, tau):
        return kvp[h, pl.ds(pl.multiple_of(ROWS * at.half + TILE * tau, TILE), 256), :]

    def far_keys(h, tau):
        return jnp.concatenate([kvc[h, tiles[tau], :], sb[h, tiles[tau], 0:TILE]], 0)

    def hot_lane(h):
        return jnp.where(lanes((TILE, TILE)) == gate_lane(h), 1.0, 0.0).astype(BF)

    def attend(n, taus, far, table):
        done = []
        for tau in taus:
            q = (qc if far else qp)[n, tiles[tau], :]
            for par in range(2):
                h = 2 * n + par
                query = only(q, par == 1)
                if far:
                    kv = far_keys(h, tau)
                    gate = jnp.concatenate([jnp.zeros((TILE, TILE), BF), sb[h, tiles[tau], TILE : 2 * TILE]], 0)
                    scores = nt(jnp.concatenate([kv, gate], 1), jnp.concatenate([query, hot_lane(h)], 1))
                else:
                    kv = near_keys(h, tau)
                    scores = nt(kv, query)
                shares = soft(scores, table)
                done.append((h, tau, shares, tn(shares, kv)))
        for k, (h, tau, shares, got) in enumerate(done):
            hid[shares_at(h, tau + (4 if far else 0))] = shares
            if h % 2:
                (atc if far else atp)[n, tiles[tau], :] = jnp.where(low_lanes, done[k - 1][3], got).astype(BF)

    def pick(h):
        for tau in range(4):
            r = 8 * (h % 3) + 2 * tau
            cut = columns[h // 3]
            col = jnp.concatenate(
                [jnp.broadcast_to(cut[0:HD, r + k : r + k + 1], (HD, TILE)) for k in range(2)], 0
            )
            for k in range(8):
                oh[tiles[tau], 128 * k : 128 * k + 128] = jnp.where(col == lanes((TILE, TILE)) + 128 * k, 1.0, 0.0).astype(BF)
        table = jnp.concatenate([kvp[h, TILE : TILE + UNIT, :], gp[...]], 1)
        for r in range(0, ROWS, 256):
            sb[h, r : r + 256, :] = nn(oh[r : r + 256, :], table).astype(BF)

    for n in range(3):
        attend(n, (1, 2, 3), False, bias[0])
        g.tick()
    while g.now < EARLY:
        g.tick()
    over[0].wait()
    for n in range(3):
        for par in range(2):
            over[1 + 2 * n + par].wait()
        attend(n, (0,), False, bias[1])
        for par in range(2):
            pick(2 * n + par)
        attend(n, (0, 1, 2, 3), True, bias[2])
        g.tick()
    pt_save = pltpu.make_async_copy(hid, pt_h, ls.at[0])
    pt_save.start()

    for n in range(3):
        a, b = atp[n], atc[n]
        att[at.c, n] = a * fb + b * nb
        atp[n] = a * nb + b * fb
    back = put(atp, att.at[at.c], es.at[13], er.at[13], at.pair)
    back.start()
    g.ready(1, 3)
    gwt[...] = jnp.concatenate([gb[t].reshape(D, 256)[:, 0:192] for t in range(TP)], 1)
    back.wait()
    for r in range(0, ROWS, 256):
        branch = nt(
            jnp.concatenate([att[k, n, r : r + 256, :] for k in range(2) for n in range(3)], 1), gwt[...]
        )
        kept = tok[r : r + 256, :].astype(F32) + branch
        resid[r : r + 256, :] = kept
        low = (layer_norm(kept)[0] * gain_two).astype(BF)
        second[r : r + 256, :] = low
        for q in (r, r + 128):
            for cut in tiles:
                xt1[cut, q : q + 128] = low[q - r : q - r + 128, cut].astype(F32).T.astype(BF)
    pt_save.wait()

    def produce(i, p, s, t):
        lhs = (xt1, xt0, xt1, xt0)[p] if p < 4 else None
        if p == 3:
            rhs = hid[t]
        elif p == 2:
            rhs = dg[t]
        elif p == 0:
            rhs = gm[t]
        elif p == 1:
            whole = jnp.concatenate([att[k, n] for k in range(2) for n in range(3)], 1)
            rhs = jnp.concatenate([whole[:, 0:192], jnp.zeros((ROWS, 64), BF)], 1)
            for o in range(1, 4):
                cut = jnp.concatenate([whole[:, 192 * o : 192 * o + 192], jnp.zeros((ROWS, 64), BF)], 1)
                rhs = jnp.where(t == o, cut, rhs)
        for k in range(8):
            block = cols[96 * k : 96 * k + 96, :] if p == 4 else nn(lhs[96 * k : 96 * k + 96, :], rhs)
            w[i % SLOTS, k // 2, k % 2, :, 0 : block.shape[1]] = block.astype(BF)

    red = Reduce(at, produce, grads, (w, rc, rh, rd, (rz0, rz1, rz2, rz3, rz4), ss, rs, rzs, rzr))

    for s in range(TP):
        g.ready(2, s)
        t = g.slot(s)
        weight = gc[t].reshape(D, 768)
        for r in range(0, ROWS, 256):
            v = nn(second[r : r + 256, :], weight)
            square = v * v
            th = jnp.tanh(GELU * (v + CUBE * v * square))
            half = 0.5 * (1.0 + th)
            hid[t, r : r + 256, :] = (v * half).astype(BF)
            slope_of = half + 0.5 * v * (1.0 - th * th) * (GELU * (1.0 + 3.0 * CUBE * square))
            dg[t, r : r + 256, :] = slope_of.astype(BF)
    for s in range(TP):
        red.tick()
        g.ready(3, s)
        t = g.slot(s)
        weight = gd[t].reshape(D, 768)
        for r in range(0, ROWS, 256):
            rows = slice(r, r + 256)
            wide[rows, :] = (resid if s == 0 else wide)[rows, :] + nt(hid[t, rows, :], weight)
            got = nn(cot[rows, :], weight)
            dg[t, rows, :] = (got * dg[t, rows, :].astype(F32)).astype(BF)
    out_save = pltpu.make_async_copy(wide, out_h, ls.at[1])
    out_save.start()
    pt_load = pltpu.make_async_copy(pt_h, hid, ls.at[2])
    pt_load.start()
    g.drain()
    out_save.wait()
    for t in range(TP):
        for r in range(0, ROWS, 256):
            rows = slice(r, r + 256)
            got = nt(dg[t, rows, :], gc[t].reshape(D, 768))
            wide[rows, :] = got if t == 0 else wide[rows, :] + got
    part_two = jnp.zeros((1, D), F32)
    for r in range(0, ROWS, 128):
        rows = slice(r, r + 128)
        got = wide[rows, :]
        normed, inverse = layer_norm(resid[rows, :])
        part_two += jnp.sum(got * normed, 0, keepdims=True)
        grad_back = cot[rows, :].astype(F32) + norm_back(got, normed, inverse, gain_two)
        wide[rows, :] = grad_back
        low = grad_back.astype(BF)
        second[rows, :] = low
        for cut in tiles:
            xt0[cut, rows] = grad_back[:, cut].T.astype(BF)
    gatt = atpc
    for r in range(0, ROWS, 256):
        grad_att = nn(second[r : r + 256, :], gwt[...]).astype(BF)
        for k in range(2):
            for n in range(3):
                gatt[k, n, r : r + 256, :] = grad_att[:, tiles[3 * k + n]]
    swap = put(gatt.at[1 - at.c], gattr, es.at[14], er.at[14], at.pair)
    swap.start()
    gacc[...] = jnp.zeros_like(gacc)
    red.tick()
    pt_load.wait()
    swap.wait()
    for n in range(3):
        a, b = gatt[at.c, n], gattr[n]
        gatt[at.c, n] = a * fb + b * nb
        gattr[n] = a * nb + b * fb

    over = []

    def slope(shares, kv, up):
        spread = nt(kv, up)
        p = shares.astype(F32)
        prod = p * spread
        return (prod - p * jnp.sum(prod, 0, keepdims=True)).astype(BF)

    def far_back(n):
        done = []
        for tau in range(4):
            q, up_pair = qc[n, tiles[tau], :], gattr[n, tiles[tau], :]
            for par in range(2):
                h = 2 * n + par
                kv = far_keys(h, tau)
                up = only(up_pair, par == 0)
                shares = hid[shares_at(h, 4 + tau)]
                down = slope(shares, kv, up)
                rhs = jnp.concatenate(
                    [jnp.concatenate([only(q, par == 1), hot_lane(h)], 1), jnp.concatenate([up, jnp.zeros_like(up)], 1)], 0
                )
                done.append((h, tau, nn(jnp.concatenate([down, shares], 1), rhs), tn(down, kv)))
        for k, (h, tau, grad, dq) in enumerate(done):
            kvc[h, tiles[tau], :] = grad[0:TILE, 0:TILE].astype(BF)
            dsel[h % 2, tiles[tau], :] = grad[TILE:256, :].astype(BF)
            if h % 2:
                qc[n, tiles[tau], :] = (jnp.where(low_lanes, dq, done[k - 1][3]) * 0.125).astype(BF)

    def near_back(n):
        done = []
        for tau in range(4):
            q, up_pair = qp[n, tiles[tau], :], gatt[at.c, n, tiles[tau], :]
            for par in range(2):
                h = 2 * n + par
                kv = near_keys(h, tau)
                up = only(up_pair, par == 0)
                shares = hid[shares_at(h, tau)]
                down = slope(shares, kv, up)
                grad = nn(jnp.concatenate([down, shares], 1), jnp.concatenate([only(q, par == 1), up], 0))
                done.append((h, tau, grad, tn(down, kv)))
        for k, (h, tau, grad, dq) in enumerate(done):
            start = pl.multiple_of(ROWS * at.half + TILE * tau, TILE)
            acc[h % 2, pl.ds(start, 256), :] += grad
            if h % 2:
                qp[n, tiles[tau], :] = (jnp.where(low_lanes, dq, done[k - 1][3]) * 0.125).astype(BF)

    def scatter(h):
        for tau in range(4):
            r = (h % 3) * 4 + tau
            chosen = jnp.broadcast_to(selrow[h // 3, r : r + 1, :], (TILE, TILE))
            for k in range(8):
                oh[tiles[k % 4], 512 * (k // 4) + 128 * tau : 512 * (k // 4) + 128 * tau + 128] = jnp.where(
                    chosen == lax.broadcasted_iota(jnp.int32, (TILE, TILE), 0) + 128 * k, 1.0, 0.0
                ).astype(BF)
        acc[h % 2, 0:TILE, :] = jnp.zeros((TILE, TILE), F32)
        for r in range(0, UNIT, 256):
            got = nn(oh[r % 512 : r % 512 + 256, 512 * (r // 512) : 512 * (r // 512) + 512], dsel[h % 2])
            acc[h % 2, TILE + r : TILE + r + 256, :] = got[:, 0:TILE]
            gacc[r : r + 256, :] += got[:, TILE : 2 * TILE]

    for n in range(3):
        far_back(n)
        red.tick()
        for par in range(2):
            scatter(2 * n + par)
        near_back(n)
        for par in range(2):
            h = 2 * n + par
            kvp[h, pl.ds(other, ROWS), :] = acc[par, pl.ds(other, ROWS), :].astype(BF)
            kvp[h, pl.ds(base, ROWS), :] = acc[par, pl.ds(base, ROWS), :].astype(BF)
            over.append(put(kvp.at[h, pl.ds(other, ROWS)], come.at[h], es.at[15 + h], er.at[15 + h], at.zp))
            over[-1].start()
        red.tick()
    gaway[...] = gacc[pl.ds(pl.multiple_of(ROWS * (1 - at.half), ROWS), ROWS), :].astype(BF)
    over.append(put(gaway, gcome, es.at[21], er.at[21], at.zp))
    over[-1].start()
    while red.now < LATE:
        red.tick()
    for copy in over:
        copy.wait()
    gate = gacc[pl.ds(gate_base, ROWS), :] + gcome[...].astype(F32)

    def deal(i, lo, a, b):
        gm[2 * at.c + i, :, lo : lo + 128] = a * fb + b * nb
        gs[i, :, lo : lo + 128] = a * nb + b * fb

    for h in range(6):
        total = kvp[h, pl.ds(base, ROWS), :].astype(F32) + come[h].astype(F32)
        deal(h // 3, 128 * (h % 3), total.astype(BF), kvc[h])
    deal(0, 384, qp[0], qc[0])
    deal(1, 384, qp[2], qc[2])
    zero = jnp.zeros((ROWS, TILE), F32)
    middle, middle_c = qp[1].astype(F32), qc[1].astype(F32)
    deal(0, 512, jnp.where(left, gate, middle).astype(BF), jnp.where(left, zero, middle_c).astype(BF))
    deal(1, 512, jnp.where(left, middle, gate).astype(BF), jnp.where(left, middle_c, zero).astype(BF))
    swap = [put(gs.at[i], gm.at[2 * at.c + i], es.at[22 + i], er.at[22 + i], at.pair) for i in range(2)]
    for copy in swap:
        copy.start()
    while red.now < 12:
        red.tick()
    flipped(xt1, first)
    for copy in swap:
        copy.wait()
    for t in range(TP):
        side = left if t % 2 == 0 else jnp.logical_not(left)
        last = gm[t, :, 512:640].astype(F32)
        gm[t, :, 512:640] = jnp.where(side, last * sg[t].astype(F32), last).astype(BF)
    for t in range(TP):
        red.tick()
        for r in range(0, ROWS, 256):
            rows = slice(r, r + 256)
            got = nt(gm[t, rows, :], ga[t].reshape(D, 640))
            resid[rows, :] = got if t == 0 else resid[rows, :] + got
    part_one = jnp.zeros((1, D), F32)
    for r in range(0, ROWS, 128):
        rows = slice(r, r + 128)
        got = resid[rows, :]
        normed, inverse = layer_norm(tok[rows, :].astype(F32))
        part_one += jnp.sum(got * normed, 0, keepdims=True)
        wide[rows, :] += norm_back(got, normed, inverse, gain_one)
    gin_save = pltpu.make_async_copy(wide, gin_h, ls.at[3])
    gin_save.start()
    cols[...] = jnp.concatenate([part_one, part_two, jnp.zeros((TILE - 2, D), F32)], 0).T
    red.finish()
    gin_save.wait()


def layer(tok, cot, w_qkv, w_score, w_out, w_fc, w_proj, gain_rows, sel, holder, inner):
    dma = pltpu.SemaphoreType.DMA
    V = pltpu.VMEM
    vm = pl.BlockSpec(memory_space=pltpu.VMEM)
    anyw = pl.BlockSpec(memory_space=pl.ANY)
    wide = V((TP, ROWS, 768), BF)
    sq, flip = V((ROWS, D), BF), V((D, ROWS), BF)
    three, six = V((3, ROWS, TILE), BF), V((6, ROWS, TILE), BF)
    picks = V((2, 24, HD), jnp.int32)
    scratch = [V((TP, 4, 2, 96, c), BF) for c in COLS] + [
        V((96, WIDE), BF), sq, V((TP, ROWS, 640), BF), V((2, ROWS, 640), BF), V((TP, ROWS, TILE), BF),
        V((TP, 8, 3, HD), jnp.int32), V((2, 8, 3, HD), jnp.int32), picks, V((2, 16, TILE), jnp.int32),
        V((6, TILE + UNIT, TILE), BF), six, three, three, V((UNIT, TILE), BF), V((6, ROWS, 2 * TILE), BF),
        V((ROWS, UNIT), BF), V((3, 256, TILE), F32), V((2, 3, ROWS, TILE), BF),
        V((2, 3, ROWS, TILE), BF), V((ROWS, D), F32), sq, wide, wide, V((D, D), BF), V((8, D), F32), V((ROWS, D), F32),
        flip, flip, three, V((2, TILE + UNIT, TILE), F32), V((UNIT, TILE), F32), V((2, ROWS, 2 * TILE), BF), six,
        V((ROWS, TILE), BF), V((ROWS, TILE), BF), V((D, TILE), F32),
        V((SLOTS, 4, 2, 96, 768), BF), V((4, 4, 96, 768), BF), V((4, 2, 48, 768), BF), V((4, 2, 96, 768), BF),
    ] + [V((3, 96, c), BF) for c in COLS + (TILE,)] + [
        dma((4, 3)), dma((4, 3)), dma((4, 4, 5)), dma((4, 4, 5)), dma((24,)), dma((24,)), dma((4,)),
        dma((SLOTS, 5)), dma((4, 5)), dma((5, 3)), dma((5, 3)),
    ]
    return pl.pallas_call(
        functools.partial(layer_kernel, inner),
        out_shape=[
            jax.ShapeDtypeStruct((ROWS, D), F32), jax.ShapeDtypeStruct((ROWS, D), F32),
            jax.ShapeDtypeStruct((96, ALL), F32), jax.ShapeDtypeStruct((TP, ROWS, 768), BF),
        ],
        in_specs=[vm] * 9 + [pl.BlockSpec(memory_space=pltpu.SMEM)],
        out_specs=[anyw, anyw, vm, anyw],
        scratch_shapes=scratch,
        compiler_params=pltpu.CompilerParams(collective_id=0, has_side_effects=True, vmem_limit_bytes=64 << 20),
    )(tok, cot, w_qkv, w_score, w_out, w_fc, w_proj, gain_rows, sel, holder)


def unpacked(grads):
    odd = lax.axis_index("tp") % 2 == 1
    piece = [grads[:, 64 * k : 64 * k + 64] for k in range(10)]
    even_cols = [7, 1, 0, 6, 2, 3, 9, 5, 4]
    odd_cols = [8, 0, 1, 7, 3, 2, 6, 4, 5]
    qkv = jnp.where(
        odd, jnp.concatenate([piece[k] for k in odd_cols], 1), jnp.concatenate([piece[k] for k in even_cols], 1)
    )
    extra = jnp.where(odd, piece[9], piece[8])
    return (
        qkv, extra[:, 0:3], grads[:, 640:832].T, grads[:, 896:1664], grads[:, 1664:2432].T, grads[:, WIDE], grads[:, WIDE + 1]
    )


def per_device(
    tokens, w_qkv, w_score, w_out, w_fc, w_proj, ln1_gain, ln2_gain, selected, holder, cotangent
):
    inner = lax.axis_size("dp") // 8
    gain_rows = jnp.stack([ln1_gain, ln2_gain])
    groups = [[o * inner + i for i in range(inner)] for o in range(8)]
    if inner > 1:
        def whole(block, axis):
            return lax.all_gather(block, "dp", axis=axis, tiled=True, axis_index_groups=groups)

        w_qkv, w_score, w_fc = whole(w_qkv, 0), whole(w_score, 0), whole(w_fc, 0)
        w_out, w_proj, gain_rows = whole(w_out, 1), whole(w_proj, 1), whole(gain_rows, 1)
    out, grad_in, grads, _ = layer(
        tokens, cotangent, w_qkv, w_score, w_out, w_fc, w_proj, gain_rows, selected, holder, inner
    )
    if inner > 1:
        grads = lax.psum_scatter(grads, "dp", scatter_dimension=0, tiled=True, axis_index_groups=groups)
    return (out, grad_in) + unpacked(grads)


def solution(mesh):
    rows = P(("dp", "tp"), None)
    cols, flip = P("dp", "tp"), P("tp", "dp")
    return jax.shard_map(
        per_device,
        mesh=mesh,
        in_specs=(rows, cols, cols, flip, cols, flip, P("dp"), P("dp"), P("dp", "tp", None), P(), rows),
        out_specs=(rows, rows, cols, cols, flip, cols, flip, P("dp"), P("dp")),
        check_vma=False,
    )
```

```python
import functools
import math

import jax
import jax.numpy as jnp
from jax import lax
from jax.experimental import pallas as pl
from jax.experimental.pallas import tpu as pltpu
from jax.sharding import PartitionSpec as P

MESH = pl.DeviceIdType.MESH
BF = jnp.bfloat16
F32 = jnp.float32
D = 768
HD = 64
COLS = (640, 256, 768, 768)
OFF = (0, 640, 896, 1664)
WIDE = 2432
ALL = 2560
TP = 4
ROWS = 512
UNIT = 1024
TILE = 128
EPS = 1e-05
FAR_OFF = -1e30
GELU = 0.7978845608
CUBE = 0.044715
RING = 6
LAG = (1, 3, 5)
EARLY = 10
ZPLAN = (-2, 0, 2, 5)
AHEAD = (1, 1, 1, 1)
LATE = 11


def nn(left, right):
    return jnp.dot(left, right, preferred_element_type=F32)


def nt(left, right):
    return lax.dot_general(left, right, (((1,), (1,)), ((), ())), preferred_element_type=F32)


def tn(left, right):
    return lax.dot_general(left, right, (((0,), (0,)), ((), ())), preferred_element_type=F32)


class Place:
    def __init__(self, inner):
        self.inner = inner
        self.dp = lax.axis_index("dp")
        self.z = lax.axis_index("tp")
        self.k = self.dp // inner
        self.cb = self.k % 2
        self.yx = self.k // 2
        self.core = (self.flip(1), self.z)
        self.xn = (self.flip(2), self.z)
        self.yn = (self.flip(4), self.z)
        self.c = self.dp % 2
        self.pair = (self.dp + 1 - 2 * self.c, self.z)
        self.half = self.z % 2
        self.zp = (self.dp, self.z + 1 - 2 * self.half)
        self.x_yx = self.yx + 1 - 2 * (self.yx % 2)
        self.y_yx = self.yx + 2 - 4 * (self.yx // 2)
        self.d_yx = 3 - self.yx

    def flip(self, bit):
        on = self.k // bit % 2
        return self.dp + (1 - 2 * on) * bit * self.inner

    def zdev(self, s):
        return (self.dp, (self.z + s) % TP)

    def barrier(self):
        devices = [self.core, self.xn, self.yn] + [self.zdev(s) for s in (1, 2, 3)]
        if self.inner > 1:
            devices.append(self.pair)
        sem = pltpu.get_barrier_semaphore()
        for device in devices:
            pl.semaphore_signal(sem, inc=1, device_id=device, device_id_type=MESH)
        pl.semaphore_wait(sem, len(devices))


def put(src, dst, send, recv, device):
    return pltpu.make_async_remote_copy(
        src_ref=src, dst_ref=dst, send_sem=send, recv_sem=recv, device_id=device, device_id_type=MESH
    )


class Gather:
    def __init__(self, at, own, bufs, sems):
        self.at, self.own, self.bufs = at, own, bufs
        self.zs, self.zr, self.ps, self.pr = sems
        self.order = [(p, s) for p in range(4) for s in range(4)]
        self.now = -1

    def slot(self, s):
        return (self.at.z - s + TP) % TP

    def along_z(self, p, s):
        a = self.at
        return put(
            self.own[p], self.bufs[p].at[a.z, a.yx, a.cb], self.zs.at[p, s - 1], self.zr.at[p, s - 1], a.zdev(s)
        )

    def along_xy(self, p, s, j):
        a = self.at
        ref = self.bufs[p].at[self.slot(s), a.yx, a.cb]
        return put(ref, ref, self.ps.at[p, s, j], self.pr.at[p, s, j], (a.xn, a.yn)[j])

    def forward(self, p, s, j):
        a = self.at
        ref = self.bufs[p].at[self.slot(s), (a.x_yx, a.y_yx)[j], a.cb, pl.ds(j * 48, 48)]
        return put(ref, ref, self.ps.at[p, s, 2 + j], self.pr.at[p, s, 2 + j], (a.yn, a.xn)[j])

    def to_core(self, p, s):
        a = self.at
        ref = self.bufs[p].at[self.slot(s), :, a.cb]
        return put(ref, ref, self.ps.at[p, s, 4], self.pr.at[p, s, 4], a.core)

    def start_z(self, p):
        for s in (1, 2, 3):
            self.along_z(p, s).start()

    def tick(self):
        i, n = self.now, len(self.order)
        self.now += 1
        if i in ZPLAN:
            self.start_z(ZPLAN.index(i))
        for k in range(n):
            if max(k - AHEAD[k // 4], -1) == i:
                p, s = self.order[k]
                if s:
                    self.along_z(p, s).wait_recv()
                for j in (0, 1):
                    self.along_xy(p, s, j).start()
        if 0 <= i - 1 < n:
            p, s = self.order[i - 1]
            for j in (0, 1):
                self.along_xy(p, s, j).wait_recv()
                self.forward(p, s, j).start()
        if 0 <= i - 2 < n:
            p, s = self.order[i - 2]
            for j in (0, 1):
                self.forward(p, s, j).wait_recv()
            self.to_core(p, s).start()
        if 0 <= i - 3 < n:
            self.to_core(*self.order[i - 3]).wait_recv()

    def ready(self, p, s):
        while self.now <= self.order.index((p, s)) + 3:
            self.tick()

    def drain(self):
        self.ready(3, 3)
        for p, s in self.order:
            if s:
                self.along_z(p, s).wait_send()
            for j in (0, 1):
                self.along_xy(p, s, j).wait_send()
                self.forward(p, s, j).wait_send()
            self.to_core(p, s).wait_send()


def layer_norm(rows):
    center = rows - jnp.mean(rows, axis=-1, keepdims=True)
    spread = jnp.mean(center * center, axis=-1, keepdims=True)
    inverse = lax.rsqrt(spread + EPS)
    return center * inverse, inverse


def lanes(shape):
    return lax.broadcasted_iota(jnp.int32, shape, len(shape) - 1)


def halves(shape):
    return lanes(shape) < HD


def only(tile, left):
    keep = halves(tile.shape)
    return jnp.where(keep if left else jnp.logical_not(keep), tile.astype(F32), 0.0).astype(tile.dtype)


def gate_lane(head):
    return head if head < 3 else HD + head - 3


class Reduce:
    def __init__(self, at, produce, result, refs):
        self.at, self.produce, self.result = at, produce, result
        self.slots, self.rc, self.rh, self.rd, self.rz, self.ss, self.rs, self.zs, self.zr = refs
        self.order = [(p, s) for p in (3, 2, 1, 0) for s in (1, 2, 3, 0)] + [(4, 0)]
        self.wide = COLS + (TILE,)
        self.off = OFF + (WIDE,)
        self.places = [0, 1, 2, 3] + list(range(5, 13)) + [0, 1, 2, 3, 4]
        self.now = 0

    def slot(self, i):
        return (self.at.z + self.order[i][1]) % TP

    def width(self, i):
        return self.wide[self.order[i][0]]

    def copy(self, i, j, src, dst, device):
        return put(src, dst, self.ss.at[i, j], self.rs.at[i, j], device)

    def to_core(self, i):
        c = self.width(i)
        src = self.slots[i].at[:, 1 - self.at.cb, :, pl.ds(0, c)]
        return self.copy(i, 0, src, self.rc.at[i % 4, :, :, pl.ds(0, c)], self.at.core)

    def diagonal(self, i, j):
        a, c = self.at, self.width(i)
        src = self.slots[i].at[a.d_yx, a.cb, pl.ds(48 * j, 48), pl.ds(0, c)]
        return self.copy(i, 1 + j, src, self.rh.at[i % RING, j, :, pl.ds(0, c)], (a.xn, a.yn)[j])

    def direct(self, i, j):
        a, c = self.at, self.width(i)
        src = self.slots[i].at[(a.x_yx, a.y_yx)[j], a.cb, :, pl.ds(0, c)]
        return self.copy(i, 3 + j, src, self.rd.at[i % RING, j, :, pl.ds(0, c)], (a.xn, a.yn)[j])

    def along_z(self, i, far=None):
        a, (p, s) = self.at, self.order[i]
        s = far or s
        src = self.slots[i].at[a.yx, a.cb, :, pl.ds(0, self.wide[p])]
        return put(src, self.rz[p].at[s - 1], self.zs.at[p, s - 1], self.zr.at[p, s - 1], a.zdev(s))

    def to_z(self, i):
        p, s = self.order[i]
        return [self.along_z(i, far) for far in ((1, 2, 3) if p == 4 else (s,) if s else ())]

    def finish_sends(self, i):
        self.to_core(i).wait_send()
        for j in (0, 1):
            self.diagonal(i, j).wait_send()
            self.direct(i, j).wait_send()
        for copy in self.to_z(i):
            copy.wait_send()

    def tick(self):
        i, n, a = self.now, len(self.order), self.at
        self.now += 1
        if i < n:
            for k in range(i):
                if self.places[k] == self.places[i]:
                    self.finish_sends(k)
            self.produce(self.slots[i], *self.order[i], self.slot(i))
            self.to_core(i).start()
        k = i - LAG[0]
        if 0 <= k < n:
            c, w = self.width(k), self.slots[k]
            self.to_core(k).wait_recv()
            for q in (a.d_yx, a.x_yx, a.y_yx, a.yx):
                w[q, a.cb, :, 0:c] = (w[q, a.cb, :, 0:c].astype(F32) + self.rc[k % 4, q, :, 0:c].astype(F32)).astype(BF)
                if q is a.d_yx:
                    for j in (0, 1):
                        self.diagonal(k, j).start()
        k = i - LAG[1]
        if 0 <= k < n:
            c, w = self.width(k), self.slots[k]
            for j in (0, 1):
                self.diagonal(k, j).wait_recv()
                q, rows = (a.y_yx, a.x_yx)[j], pl.ds(48 * j, 48)
                w[q, a.cb, rows, 0:c] = (
                    w[q, a.cb, rows, 0:c].astype(F32) + self.rh[k % RING, j, :, 0:c].astype(F32)
                ).astype(BF)
                self.direct(k, 1 - j).start()
        k = i - LAG[2]
        if 0 <= k < n:
            w = self.slots[k]
            p, s = self.order[k]
            c = self.wide[p]
            for j in (0, 1):
                self.direct(k, j).wait_recv()
            total = (
                w[a.yx, a.cb, :, 0:c].astype(F32)
                + self.rd[k % RING, 0, :, 0:c].astype(F32)
                + self.rd[k % RING, 1, :, 0:c].astype(F32)
            )
            if s or p == 4:
                w[a.yx, a.cb, :, 0:c] = total.astype(BF)
                for copy in self.to_z(k):
                    copy.start()
            if not s:
                self.result[:, self.off[p] : self.off[p] + c] = total

    def finish(self):
        n = len(self.order)
        while self.now < n + LAG[2]:
            self.tick()
        for i in range(4, n):
            self.finish_sends(i)
        for p in (3, 2, 1, 0, 4):
            for s in (1, 2, 3):
                self.along_z(self.order.index((p, 0 if p == 4 else s)), s).wait_recv()
            lo, c = self.off[p], self.wide[p]
            self.result[:, lo : lo + c] += (
                self.rz[p][0].astype(F32) + self.rz[p][1].astype(F32) + self.rz[p][2].astype(F32)
            )


def norm_back(grad, normed, inverse, gain):
    inner = grad * gain
    return inverse * (
        inner - jnp.mean(inner, -1, keepdims=True) - normed * jnp.mean(inner * normed, -1, keepdims=True)
    )


def layer_kernel(
    inner, tok, cot, w_qkv, score_rows, w_out, w_fc, proj_rows, one, two, sel, holder,
    out_h, gin_h, grads, pt_h,
    ga, gb, gc, gd, pack, first, mixed, mrecv, sg, selz, selp, selq, selrow, kvp, kvc, qp, qc, gp, sb, oh, bias, atpc,
    att, resid, second, hid, dg, gwt, gains, wide, xt0, xt1, gattr, acc, gacc, dsel, come, gaway, gcome, cols,
    w, rc, rh, rd, rz0, rz1, rz2, rz3, rz4,
    zs, zr, ps, pr, es, er, ls, ss, rs, rzs, rzr,
):
    at = Place(inner)
    bufs = (ga, gb, gc, gd)
    own = [pack.at[:, pl.ds(OFF[p], COLS[p])] for p in range(4)]
    g = Gather(at, own, bufs, (zs, zr, ps, pr))
    atp, atc, gm, gs = atpc.at[0], atpc.at[1], mixed, mrecv
    odd = at.z % 2
    tiles = [slice(128 * k, 128 * k + 128) for k in range(6)]

    def flipped(dst, src):
        for r in range(0, ROWS, 128):
            for cut in tiles:
                dst[cut, r : r + 128] = src[r : r + 128, cut].astype(F32).T.astype(BF)

    is_odd = lanes((96, TILE)) * 0 + odd == 1
    q0, k0, v0, q1, k1, v1, q2, k2, v2 = [w_qkv[:, 64 * k : 64 * k + 64].astype(F32) for k in range(9)]
    rowed = jnp.concatenate([score_rows[...].astype(F32), one[...].astype(F32), two[...].astype(F32)], 0)
    rowed = jnp.concatenate([rowed, jnp.zeros((5, 32), F32)], 1)
    extra = jnp.concatenate([rowed, jnp.zeros((TILE - 5, TILE), F32)], 0).T[0:96, 0:HD]
    even_cols = ((v0, k0), (k1, v1), (v2, k2), (q1, q0), (extra, q2))
    odd_cols = ((k0, v0), (v1, k1), (k2, v2), (q2, q1), (q0, extra))
    for k in range(5):
        tile = jnp.where(is_odd, jnp.concatenate(odd_cols[k], 1), jnp.concatenate(even_cols[k], 1)).astype(BF)
        pack[:, tiles[k]] = tile
        ga[at.z, at.yx, at.cb, :, tiles[k]] = tile
    at.barrier()
    g.start_z(0)
    g.tick()

    def blocks_of(z):
        return pl.ds(pl.multiple_of(8 * z, 8), 8)

    selz[at.z] = sel[:, blocks_of(at.z), :]
    sel_out = [
        put(sel.at[:, blocks_of((at.z + s) % TP)], selz.at[at.z], es.at[s - 1], er.at[s - 1], at.zdev(s)) for s in (1, 2, 3)
    ]
    for copy in sel_out:
        copy.start()
    flipped_out = jnp.concatenate([w_out[...].astype(F32), jnp.zeros((64, 96), F32)], 0)
    pack[:, 640:896] = flipped_out.T.astype(BF)
    pack[:, 896:1664] = w_fc[...]
    pack[:, 1664:2432] = proj_rows[...]
    for p in (1, 2, 3):
        bufs[p][at.z, at.yx, at.cb] = own[p][...]
    g.tick()
    f = jnp.full((1, TILE), jnp.where(holder[at.dp // 2 * 2 + at.z // 2] == at.c, 1.0, 0.0), F32)
    fb = f.astype(BF)
    nb = (1.0 - f).astype(BF)

    key = lax.broadcasted_iota(jnp.int32, (256, TILE), 0)
    row = lax.broadcasted_iota(jnp.int32, (256, TILE), 1)
    gap = row + TILE - key
    band = (gap >= 0) & (gap < HD)
    bias[0] = jnp.where(band, 0.0, FAR_OFF)
    reach = TILE * (1 - at.half)
    bias[1] = jnp.where(band & (key >= reach), 0.0, FAR_OFF)
    close = (row - key >= 0) & (row - key < HD)
    bias[2] = jnp.where(
        ((key < TILE) & close) | ((key >= TILE) & ((key - TILE) // HD == row // HD)), 0.0, FAR_OFF
    )
    kvp[:, 0:TILE, :] = jnp.zeros((6, TILE, TILE), BF)

    normed = layer_norm(tok[...].astype(F32))[0]
    for copy in sel_out:
        copy.wait()
    sel_core = put(selz.at[pl.ds(2 * (1 - at.c), 2)], selp, es.at[3], er.at[3], at.pair)
    sel_core.start()
    flipped(xt0, cot)
    g.ready(0, 0)
    extra = ga[at.z, :, :, :, 512:640].reshape(D, TILE).astype(F32).T
    odd_f = odd.astype(F32)
    gains[...] = extra[0:8] * (1.0 - odd_f) + extra[HD : HD + 8] * odd_f
    gain_one, gain_two = gains[3:4, :], gains[4:5, :]
    first[...] = (normed * gain_one).astype(BF)
    sel_core.wait()
    fi = f.astype(jnp.int32)[:, 0:64]
    columns = []
    for i in range(2):
        for j in range(3):
            selq[i, 8 * j : 8 * j + 8, :] = selz[2 * at.c + i, j] * (1 - fi) + selp[i, j] * fi
        both = selq[i]
        square = jnp.concatenate([both.astype(F32), jnp.zeros((104, HD), F32)], 0)
        columns.append(jnp.concatenate([square, jnp.zeros((TILE, HD), F32)], 1).T.astype(jnp.int32))
        for r in range(12):
            selrow[i, r : r + 1, :] = jnp.concatenate([both[2 * r : 2 * r + 1, :], both[2 * r + 1 : 2 * r + 2, :]], 1)

    for s in range(TP):
        g.ready(0, s)
        t = g.slot(s)
        weight = ga[t].reshape(D, 640)
        extra_side = (lanes((256, TILE)) // HD) == t % 2
        for r in range(0, ROWS, 256):
            got = nn(first[r : r + 256, :], weight)
            mixed[t, r : r + 256, 0:512] = got[:, 0:512].astype(BF)
            last = got[:, 512:640]
            soft_part = jnp.log(1.0 + jnp.exp(-jnp.abs(last)))
            mixed[t, r : r + 256, 512:640] = jnp.where(
                extra_side, jnp.minimum(last, 0.0) - soft_part, last
            ).astype(BF)
            sg[t, r : r + 256, :] = (1.0 / (1.0 + jnp.exp(last))).astype(BF)
    swap = [
        put(mixed.at[2 * (1 - at.c) + i], mrecv.at[i], es.at[4 + i], er.at[4 + i], at.pair) for i in range(2)
    ]
    for copy in swap:
        copy.start()
    g.tick()
    for copy in swap:
        copy.wait()
    base = pl.multiple_of(TILE + ROWS * at.half, TILE)
    other = pl.multiple_of(TILE + ROWS * (1 - at.half), TILE)
    gate_base = pl.multiple_of(ROWS * at.half, ROWS)
    left = halves((ROWS, TILE))
    gate_own = jnp.where(left, mixed[2 * at.c, :, 512:640].astype(F32), mixed[2 * at.c + 1, :, 512:640].astype(F32))
    gate_pair = jnp.where(left, mrecv[0, :, 512:640].astype(F32), mrecv[1, :, 512:640].astype(F32))
    wanted = (lanes((ROWS, TILE)) % HD) < 3
    gp[pl.ds(gate_base, ROWS), :] = jnp.where(wanted, gate_own * f + gate_pair * (1.0 - f), 0.0).astype(BF)
    part = gp.at[pl.ds(gate_base, ROWS)]
    over = [put(part, part, es.at[6], er.at[6], at.zp)]
    over[0].start()
    for i in range(2):
        for j in range(3):
            a = mixed[2 * at.c + i, :, tiles[j]]
            b = mrecv[i, :, tiles[j]]
            h = 3 * i + j
            kvp[h, pl.ds(base, ROWS), :] = a * fb + b * nb
            part = kvp.at[h, pl.ds(base, ROWS)]
            over.append(put(part, part, es.at[7 + h], er.at[7 + h], at.zp))
            over[-1].start()
            kvc[h] = a * nb + b * fb
    for n in range(3):
        if n == 1:
            a = jnp.where(left, mixed[2 * at.c + 1, :, 512:640].astype(F32), mixed[2 * at.c, :, 512:640].astype(F32)).astype(BF)
            b = jnp.where(left, mrecv[1, :, 512:640].astype(F32), mrecv[0, :, 512:640].astype(F32)).astype(BF)
        else:
            a = mixed[2 * at.c + n // 2, :, 384:512]
            b = mrecv[n // 2, :, 384:512]
        eighth = jnp.asarray(0.125, BF)
        qp[n] = (a * fb + b * nb) * eighth
        qc[n] = (a * nb + b * fb) * eighth
    g.tick()

    low_lanes = halves((TILE, TILE))

    def soft(scores, table):
        scores = scores + table
        top = jnp.max(scores, axis=0, keepdims=True)
        raised = jnp.exp(scores - top)
        return (raised * (1.0 / jnp.sum(raised, axis=0, keepdims=True))).astype(BF)

    def shares_at(h, tile):
        return tile // 2, slice(tile % 2 * 256, tile % 2 * 256 + 256), tiles[h]

    def near_keys(h, tau):
        return kvp[h, pl.ds(pl.multiple_of(ROWS * at.half + TILE * tau, TILE), 256), :]

    def far_keys(h, tau):
        return jnp.concatenate([kvc[h, tiles[tau], :], sb[h, tiles[tau], 0:TILE]], 0)

    def hot_lane(h):
        return jnp.where(lanes((TILE, TILE)) == gate_lane(h), 1.0, 0.0).astype(BF)

    def attend(n, taus, far, table):
        done = []
        for tau in taus:
            q = (qc if far else qp)[n, tiles[tau], :]
            for par in range(2):
                h = 2 * n + par
                query = only(q, par == 1)
                if far:
                    kv = far_keys(h, tau)
                    gate = jnp.concatenate([jnp.zeros((TILE, TILE), BF), sb[h, tiles[tau], TILE : 2 * TILE]], 0)
                    scores = nt(jnp.concatenate([kv, gate], 1), jnp.concatenate([query, hot_lane(h)], 1))
                else:
                    kv = near_keys(h, tau)
                    scores = nt(kv, query)
                shares = soft(scores, table)
                done.append((h, tau, shares, tn(shares, kv)))
        for k, (h, tau, shares, got) in enumerate(done):
            hid[shares_at(h, tau + (4 if far else 0))] = shares
            if h % 2:
                (atc if far else atp)[n, tiles[tau], :] = jnp.where(low_lanes, done[k - 1][3], got).astype(BF)

    def pick(h):
        for tau in range(4):
            r = 8 * (h % 3) + 2 * tau
            cut = columns[h // 3]
            col = jnp.concatenate(
                [jnp.broadcast_to(cut[0:HD, r + k : r + k + 1], (HD, TILE)) for k in range(2)], 0
            )
            for k in range(8):
                oh[tiles[tau], 128 * k : 128 * k + 128] = jnp.where(col == lanes((TILE, TILE)) + 128 * k, 1.0, 0.0).astype(BF)
        table = jnp.concatenate([kvp[h, TILE : TILE + UNIT, :], gp[...]], 1)
        for r in range(0, ROWS, 256):
            sb[h, r : r + 256, :] = nn(oh[r : r + 256, :], table).astype(BF)

    for n in range(3):
        attend(n, (1, 2, 3), False, bias[0])
        g.tick()
    while g.now < EARLY:
        g.tick()
    over[0].wait()
    for n in range(3):
        for par in range(2):
            over[1 + 2 * n + par].wait()
        attend(n, (0,), False, bias[1])
        for par in range(2):
            pick(2 * n + par)
        attend(n, (0, 1, 2, 3), True, bias[2])
        g.tick()
    pt_save = pltpu.make_async_copy(hid, pt_h, ls.at[0])
    pt_save.start()

    for n in range(3):
        a, b = atp[n], atc[n]
        att[at.c, n] = a * fb + b * nb
        atp[n] = a * nb + b * fb
    back = put(atp, att.at[at.c], es.at[13], er.at[13], at.pair)
    back.start()
    g.ready(1, 3)
    gwt[...] = jnp.concatenate([gb[t].reshape(D, 256)[:, 0:192] for t in range(TP)], 1)
    back.wait()
    for r in range(0, ROWS, 256):
        branch = nt(
            jnp.concatenate([att[k, n, r : r + 256, :] for k in range(2) for n in range(3)], 1), gwt[...]
        )
        kept = tok[r : r + 256, :].astype(F32) + branch
        resid[r : r + 256, :] = kept
        low = (layer_norm(kept)[0] * gain_two).astype(BF)
        second[r : r + 256, :] = low
        for q in (r, r + 128):
            for cut in tiles:
                xt1[cut, q : q + 128] = low[q - r : q - r + 128, cut].astype(F32).T.astype(BF)
    pt_save.wait()

    def produce(slot, p, s, t):
        lhs = (xt1, xt0, xt1, xt0)[p] if p < 4 else None
        if p == 3:
            rhs = hid[t]
        elif p == 2:
            rhs = dg[t]
        elif p == 0:
            rhs = gm[t]
        elif p == 1:
            whole = jnp.concatenate([att[k, n] for k in range(2) for n in range(3)], 1)
            rhs = jnp.concatenate([whole[:, 0:192], jnp.zeros((ROWS, 64), BF)], 1)
            for o in range(1, 4):
                cut = jnp.concatenate([whole[:, 192 * o : 192 * o + 192], jnp.zeros((ROWS, 64), BF)], 1)
                rhs = jnp.where(t == o, cut, rhs)
        for k in range(8):
            block = cols[96 * k : 96 * k + 96, :] if p == 4 else nn(lhs[96 * k : 96 * k + 96, :], rhs)
            slot[k // 2, k % 2, :, 0 : block.shape[1]] = block.astype(BF)

    slots = [ref.at[k] for ref in (w, gd, gc, w) for k in range(4)] + [w.at[4]]
    red = Reduce(at, produce, grads, (slots, rc, rh, rd, (rz0, rz1, rz2, rz3, rz4), ss, rs, rzs, rzr))

    for s in range(TP):
        g.ready(2, s)
        t = g.slot(s)
        weight = gc[t].reshape(D, 768)
        for r in range(0, ROWS, 256):
            v = nn(second[r : r + 256, :], weight)
            square = v * v
            th = jnp.tanh(GELU * (v + CUBE * v * square))
            half = 0.5 * (1.0 + th)
            hid[t, r : r + 256, :] = (v * half).astype(BF)
            slope_of = half + 0.5 * v * (1.0 - th * th) * (GELU * (1.0 + 3.0 * CUBE * square))
            dg[t, r : r + 256, :] = slope_of.astype(BF)
    for s in range(TP):
        red.tick()
        g.ready(3, s)
        t = g.slot(s)
        weight = gd[t].reshape(D, 768)
        for r in range(0, ROWS, 256):
            rows = slice(r, r + 256)
            wide[rows, :] = (resid if s == 0 else wide)[rows, :] + nt(hid[t, rows, :], weight)
            got = nn(cot[rows, :], weight)
            dg[t, rows, :] = (got * dg[t, rows, :].astype(F32)).astype(BF)
    out_save = pltpu.make_async_copy(wide, out_h, ls.at[1])
    out_save.start()
    pt_load = pltpu.make_async_copy(pt_h, hid, ls.at[2])
    pt_load.start()
    g.drain()
    out_save.wait()
    for t in range(TP):
        for r in range(0, ROWS, 256):
            rows = slice(r, r + 256)
            got = nt(dg[t, rows, :], gc[t].reshape(D, 768))
            wide[rows, :] = got if t == 0 else wide[rows, :] + got
    part_two = jnp.zeros((1, D), F32)
    for r in range(0, ROWS, 128):
        rows = slice(r, r + 128)
        got = wide[rows, :]
        normed, inverse = layer_norm(resid[rows, :])
        part_two += jnp.sum(got * normed, 0, keepdims=True)
        grad_back = cot[rows, :].astype(F32) + norm_back(got, normed, inverse, gain_two)
        wide[rows, :] = grad_back
        low = grad_back.astype(BF)
        second[rows, :] = low
        for cut in tiles:
            xt0[cut, rows] = grad_back[:, cut].T.astype(BF)
    gatt = atpc
    for r in range(0, ROWS, 256):
        grad_att = nn(second[r : r + 256, :], gwt[...]).astype(BF)
        for k in range(2):
            for n in range(3):
                gatt[k, n, r : r + 256, :] = grad_att[:, tiles[3 * k + n]]
    swap = put(gatt.at[1 - at.c], gattr, es.at[14], er.at[14], at.pair)
    swap.start()
    gacc[...] = jnp.zeros_like(gacc)
    red.tick()
    pt_load.wait()
    swap.wait()
    for n in range(3):
        a, b = gatt[at.c, n], gattr[n]
        gatt[at.c, n] = a * fb + b * nb
        gattr[n] = a * nb + b * fb

    over = []

    def slope(shares, kv, up):
        spread = nt(kv, up)
        p = shares.astype(F32)
        prod = p * spread
        return (prod - p * jnp.sum(prod, 0, keepdims=True)).astype(BF)

    def far_back(n):
        done = []
        for tau in range(4):
            q, up_pair = qc[n, tiles[tau], :], gattr[n, tiles[tau], :]
            for par in range(2):
                h = 2 * n + par
                kv = far_keys(h, tau)
                up = only(up_pair, par == 0)
                shares = hid[shares_at(h, 4 + tau)]
                down = slope(shares, kv, up)
                rhs = jnp.concatenate(
                    [jnp.concatenate([only(q, par == 1), hot_lane(h)], 1), jnp.concatenate([up, jnp.zeros_like(up)], 1)], 0
                )
                done.append((h, tau, nn(jnp.concatenate([down, shares], 1), rhs), tn(down, kv)))
        for k, (h, tau, grad, dq) in enumerate(done):
            kvc[h, tiles[tau], :] = grad[0:TILE, 0:TILE].astype(BF)
            dsel[h % 2, tiles[tau], :] = grad[TILE:256, :].astype(BF)
            if h % 2:
                qc[n, tiles[tau], :] = (jnp.where(low_lanes, dq, done[k - 1][3]) * 0.125).astype(BF)

    def near_back(n):
        done = []
        for tau in range(4):
            q, up_pair = qp[n, tiles[tau], :], gatt[at.c, n, tiles[tau], :]
            for par in range(2):
                h = 2 * n + par
                kv = near_keys(h, tau)
                up = only(up_pair, par == 0)
                shares = hid[shares_at(h, tau)]
                down = slope(shares, kv, up)
                grad = nn(jnp.concatenate([down, shares], 1), jnp.concatenate([only(q, par == 1), up], 0))
                done.append((h, tau, grad, tn(down, kv)))
        for k, (h, tau, grad, dq) in enumerate(done):
            start = pl.multiple_of(ROWS * at.half + TILE * tau, TILE)
            acc[h % 2, pl.ds(start, 256), :] += grad
            if h % 2:
                qp[n, tiles[tau], :] = (jnp.where(low_lanes, dq, done[k - 1][3]) * 0.125).astype(BF)

    def scatter(h):
        for tau in range(4):
            r = (h % 3) * 4 + tau
            chosen = jnp.broadcast_to(selrow[h // 3, r : r + 1, :], (TILE, TILE))
            for k in range(8):
                oh[tiles[k % 4], 512 * (k // 4) + 128 * tau : 512 * (k // 4) + 128 * tau + 128] = jnp.where(
                    chosen == lax.broadcasted_iota(jnp.int32, (TILE, TILE), 0) + 128 * k, 1.0, 0.0
                ).astype(BF)
        acc[h % 2, 0:TILE, :] = jnp.zeros((TILE, TILE), F32)
        for r in range(0, UNIT, 256):
            got = nn(oh[r % 512 : r % 512 + 256, 512 * (r // 512) : 512 * (r // 512) + 512], dsel[h % 2])
            acc[h % 2, TILE + r : TILE + r + 256, :] = got[:, 0:TILE]
            gacc[r : r + 256, :] += got[:, TILE : 2 * TILE]

    for n in range(3):
        far_back(n)
        red.tick()
        for par in range(2):
            scatter(2 * n + par)
        near_back(n)
        for par in range(2):
            h = 2 * n + par
            kvp[h, pl.ds(other, ROWS), :] = acc[par, pl.ds(other, ROWS), :].astype(BF)
            kvp[h, pl.ds(base, ROWS), :] = acc[par, pl.ds(base, ROWS), :].astype(BF)
            over.append(put(kvp.at[h, pl.ds(other, ROWS)], come.at[h], es.at[15 + h], er.at[15 + h], at.zp))
            over[-1].start()
        red.tick()
    gaway[...] = gacc[pl.ds(pl.multiple_of(ROWS * (1 - at.half), ROWS), ROWS), :].astype(BF)
    over.append(put(gaway, gcome, es.at[21], er.at[21], at.zp))
    over[-1].start()
    while red.now < LATE:
        red.tick()
    for copy in over:
        copy.wait()
    gate = gacc[pl.ds(gate_base, ROWS), :] + gcome[...].astype(F32)

    def deal(i, lo, a, b):
        gm[2 * at.c + i, :, lo : lo + 128] = a * fb + b * nb
        gs[i, :, lo : lo + 128] = a * nb + b * fb

    for h in range(6):
        total = kvp[h, pl.ds(base, ROWS), :].astype(F32) + come[h].astype(F32)
        deal(h // 3, 128 * (h % 3), total.astype(BF), kvc[h])
    deal(0, 384, qp[0], qc[0])
    deal(1, 384, qp[2], qc[2])
    zero = jnp.zeros((ROWS, TILE), F32)
    middle, middle_c = qp[1].astype(F32), qc[1].astype(F32)
    deal(0, 512, jnp.where(left, gate, middle).astype(BF), jnp.where(left, zero, middle_c).astype(BF))
    deal(1, 512, jnp.where(left, middle, gate).astype(BF), jnp.where(left, middle_c, zero).astype(BF))
    swap = [put(gs.at[i], gm.at[2 * at.c + i], es.at[22 + i], er.at[22 + i], at.pair) for i in range(2)]
    for copy in swap:
        copy.start()
    while red.now < 12:
        red.tick()
    flipped(xt1, first)
    for copy in swap:
        copy.wait()
    for t in range(TP):
        side = left if t % 2 == 0 else jnp.logical_not(left)
        last = gm[t, :, 512:640].astype(F32)
        gm[t, :, 512:640] = jnp.where(side, last * sg[t].astype(F32), last).astype(BF)
    for t in range(TP):
        red.tick()
        for r in range(0, ROWS, 256):
            rows = slice(r, r + 256)
            got = nt(gm[t, rows, :], ga[t].reshape(D, 640))
            resid[rows, :] = got if t == 0 else resid[rows, :] + got
    part_one = jnp.zeros((1, D), F32)
    for r in range(0, ROWS, 128):
        rows = slice(r, r + 128)
        got = resid[rows, :]
        normed, inverse = layer_norm(tok[rows, :].astype(F32))
        part_one += jnp.sum(got * normed, 0, keepdims=True)
        wide[rows, :] += norm_back(got, normed, inverse, gain_one)
    gin_save = pltpu.make_async_copy(wide, gin_h, ls.at[3])
    gin_save.start()
    cols[...] = jnp.concatenate([part_one, part_two, jnp.zeros((TILE - 2, D), F32)], 0).T
    red.finish()
    gin_save.wait()


def layer(tok, cot, w_qkv, score_rows, w_out, w_fc, proj_rows, one, two, sel, holder, inner):
    dma = pltpu.SemaphoreType.DMA
    V = pltpu.VMEM
    vm = pl.BlockSpec(memory_space=pltpu.VMEM)
    anyw = pl.BlockSpec(memory_space=pl.ANY)
    wide = V((TP, ROWS, 768), BF)
    sq, flip = V((ROWS, D), BF), V((D, ROWS), BF)
    three, six = V((3, ROWS, TILE), BF), V((6, ROWS, TILE), BF)
    picks = V((2, 24, HD), jnp.int32)
    scratch = [V((TP, 4, 2, 96, c), BF) for c in COLS] + [
        V((96, WIDE), BF), sq, V((TP, ROWS, 640), BF), V((2, ROWS, 640), BF), V((TP, ROWS, TILE), BF),
        V((TP, 3, 8, HD), jnp.int32), V((2, 3, 8, HD), jnp.int32), picks, V((2, 16, TILE), jnp.int32),
        V((6, TILE + UNIT, TILE), BF), six, three, three, V((UNIT, TILE), BF), V((6, ROWS, 2 * TILE), BF),
        V((ROWS, UNIT), BF), V((3, 256, TILE), F32), V((2, 3, ROWS, TILE), BF),
        V((2, 3, ROWS, TILE), BF), V((ROWS, D), F32), sq, wide, wide, V((D, D), BF), V((8, D), F32), V((ROWS, D), F32),
        flip, flip, three, V((2, TILE + UNIT, TILE), F32), V((UNIT, TILE), F32), V((2, ROWS, 2 * TILE), BF), six,
        V((ROWS, TILE), BF), V((ROWS, TILE), BF), V((D, TILE), F32),
        V((5, 4, 2, 96, 768), BF), V((4, 4, 96, 768), BF), V((RING, 2, 48, 768), BF), V((RING, 2, 96, 768), BF),
    ] + [V((3, 96, c), BF) for c in COLS + (TILE,)] + [
        dma((4, 3)), dma((4, 3)), dma((4, 4, 5)), dma((4, 4, 5)), dma((24,)), dma((24,)), dma((4,)),
        dma((17, 5)), dma((17, 5)), dma((5, 3)), dma((5, 3)),
    ]
    return pl.pallas_call(
        functools.partial(layer_kernel, inner),
        out_shape=[
            jax.ShapeDtypeStruct((ROWS, D), F32), jax.ShapeDtypeStruct((ROWS, D), F32),
            jax.ShapeDtypeStruct((96, ALL), F32), jax.ShapeDtypeStruct((TP, ROWS, 768), BF),
        ],
        in_specs=[vm] * 10 + [pl.BlockSpec(memory_space=pltpu.SMEM)],
        out_specs=[anyw, anyw, vm, anyw],
        scratch_shapes=scratch,
        compiler_params=pltpu.CompilerParams(collective_id=0, has_side_effects=True, vmem_limit_bytes=64 << 20),
    )(tok, cot, w_qkv, score_rows, w_out, w_fc, proj_rows, one, two, sel, holder)


EVEN = (7, 1, 0, 6, 2, 3, 9, 5, 4)
ODD = (8, 0, 1, 7, 3, 2, 6, 4, 5)


def finish_kernel(out_h, gin_h, grads, out, gin, qkv, score, w_out, fc, proj, one, two, sems):
    copies = [pltpu.make_async_copy(a, b, sems.at[k]) for k, (a, b) in enumerate(((out_h, out), (gin_h, gin)))]
    for copy in copies:
        copy.start()
    odd = lax.axis_index("tp") % 2
    is_odd = lanes((96, HD)) * 0 + odd == 1
    piece = [grads[:, 64 * k : 64 * k + 64] for k in range(10)]
    for k in range(9):
        qkv[:, 64 * k : 64 * k + 64] = jnp.where(is_odd, piece[ODD[k]], piece[EVEN[k]])
    extra = jnp.concatenate([jnp.where(is_odd, piece[9], piece[8]), grads[:, WIDE : WIDE + HD]], 1)
    score[...] = jnp.concatenate([extra, jnp.zeros((32, TILE), F32)], 0).T[0:3, 0:96]
    fc[...] = grads[:, 896:1664]

    def turned(lo, hi):
        return jnp.concatenate([grads[:, lo:hi], jnp.zeros((32, hi - lo), F32)], 0).T[:, 0:96]

    w_out[...] = turned(640, 896)[0:192, :]
    proj[...] = grads[:, 1664:2432]
    gain = turned(WIDE, ALL)
    one[...] = gain[0:1, :]
    two[...] = gain[1:2, :]
    for copy in copies:
        copy.wait()


def finished(out, grad_in, grads):
    vm = pl.BlockSpec(memory_space=pltpu.VMEM)
    anyw = pl.BlockSpec(memory_space=pl.ANY)
    shapes = ((ROWS, D), (ROWS, D), (96, 576), (3, 96), (192, 96), (96, 768), (96, 768), (1, 96), (1, 96))
    got = pl.pallas_call(
        finish_kernel,
        out_shape=[jax.ShapeDtypeStruct(s, F32) for s in shapes],
        in_specs=[vm] * 3,
        out_specs=[anyw, anyw] + [vm] * 7,
        scratch_shapes=[pltpu.SemaphoreType.DMA((2,))],
        compiler_params=pltpu.CompilerParams(vmem_limit_bytes=60 << 20),
    )(out, grad_in, grads)
    out, gin, qkv, score, w_out, fc, proj, one, two = got
    return out, gin, qkv, score.T, w_out, fc, proj.T, one.reshape(96), two.reshape(96)


def unpacked(grads):
    odd = lax.axis_index("tp") % 2 == 1
    piece = [grads[:, 64 * k : 64 * k + 64] for k in range(10)]
    qkv = jnp.where(
        odd, jnp.concatenate([piece[k] for k in ODD], 1), jnp.concatenate([piece[k] for k in EVEN], 1)
    )
    extra = jnp.where(odd, piece[9], piece[8])
    return (
        qkv, extra[:, 0:3], grads[:, 640:832].T, grads[:, 896:1664], grads[:, 1664:2432].T, grads[:, WIDE], grads[:, WIDE + 1]
    )


def per_device(
    tokens, w_qkv, w_score, w_out, w_fc, w_proj, ln1_gain, ln2_gain, selected, holder, cotangent
):
    inner = lax.axis_size("dp") // 8
    one, two = ln1_gain.reshape(1, -1), ln2_gain.reshape(1, -1)
    score_rows, proj_rows = w_score.T, w_proj.T
    groups = [[o * inner + i for i in range(inner)] for o in range(8)]
    if inner > 1:
        def whole(block, axis):
            return lax.all_gather(block, "dp", axis=axis, tiled=True, axis_index_groups=groups)

        w_qkv, w_fc = whole(w_qkv, 0), whole(w_fc, 0)
        w_out, proj_rows, score_rows, one, two = (
            whole(w_out, 1), whole(proj_rows, 0), whole(score_rows, 1), whole(one, 1), whole(two, 1)
        )
    out, grad_in, grads, _ = layer(
        tokens, cotangent, w_qkv, score_rows, w_out, w_fc, proj_rows, one, two, selected.transpose(1, 0, 2), holder, inner
    )
    if inner == 1:
        return finished(out, grad_in, grads)
    grads = lax.psum_scatter(grads, "dp", scatter_dimension=0, tiled=True, axis_index_groups=groups)
    return (out, grad_in) + unpacked(grads)


def solution(mesh):
    rows = P(("dp", "tp"), None)
    cols, flip = P("dp", "tp"), P("tp", "dp")
    return jax.shard_map(
        per_device,
        mesh=mesh,
        in_specs=(rows, cols, cols, flip, cols, flip, P("dp"), P("dp"), P("dp", "tp", None), P(), rows),
        out_specs=(rows, rows, cols, cols, flip, cols, flip, P("dp"), P("dp")),
        check_vma=False,
    )
```

```python
import functools
import math

import jax
import jax.numpy as jnp
from jax import lax
from jax.experimental import pallas as pl
from jax.experimental.pallas import tpu as pltpu
from jax.sharding import PartitionSpec as P

MESH = pl.DeviceIdType.MESH
BF = jnp.bfloat16
F32 = jnp.float32
D = 768
HD = 64
COLS = (640, 256, 768, 768)
OFF = (0, 640, 896, 1664)
WIDE = 2432
ALL = 2560
TP = 4
ROWS = 512
UNIT = 1024
TILE = 128
EPS = 1e-05
FAR_OFF = -1e30
GELU = 0.7978845608
CUBE = 0.044715
RING = 6
PUSH = 0
LAG = (1, 3, 5)
EARLY = 10
ZPLAN = (-2, 0, 2, 5)
AHEAD = (1, 1, 1, 1)
LATE = 11


def nn(left, right):
    return jnp.dot(left, right, preferred_element_type=F32)


def nt(left, right):
    return lax.dot_general(left, right, (((1,), (1,)), ((), ())), preferred_element_type=F32)


def tn(left, right):
    return lax.dot_general(left, right, (((0,), (0,)), ((), ())), preferred_element_type=F32)


class Place:
    def __init__(self, inner):
        self.inner = inner
        self.dp = lax.axis_index("dp")
        self.z = lax.axis_index("tp")
        self.k = self.dp // inner
        self.cb = self.k % 2
        self.yx = self.k // 2
        self.core = (self.flip(1), self.z)
        self.xn = (self.flip(2), self.z)
        self.yn = (self.flip(4), self.z)
        self.c = self.dp % 2
        self.pair = (self.dp + 1 - 2 * self.c, self.z)
        self.half = self.z % 2
        self.zp = (self.dp, self.z + 1 - 2 * self.half)
        self.x_yx = self.yx + 1 - 2 * (self.yx % 2)
        self.y_yx = self.yx + 2 - 4 * (self.yx // 2)
        self.d_yx = 3 - self.yx

    def flip(self, bit):
        on = self.k // bit % 2
        return self.dp + (1 - 2 * on) * bit * self.inner

    def zdev(self, s):
        return (self.dp, (self.z + s) % TP)

    def barrier(self):
        devices = [self.core, self.xn, self.yn] + [self.zdev(s) for s in (1, 2, 3)]
        if self.inner > 1:
            devices.append(self.pair)
        sem = pltpu.get_barrier_semaphore()
        for device in devices:
            pl.semaphore_signal(sem, inc=1, device_id=device, device_id_type=MESH)
        pl.semaphore_wait(sem, len(devices))


def put(src, dst, send, recv, device):
    return pltpu.make_async_remote_copy(
        src_ref=src, dst_ref=dst, send_sem=send, recv_sem=recv, device_id=device, device_id_type=MESH
    )


class Gather:
    def __init__(self, at, own, bufs, sems):
        self.at, self.own, self.bufs = at, own, bufs
        self.zs, self.zr, self.ps, self.pr = sems
        self.order = [(p, s) for p in range(4) for s in range(4)]
        self.now = -1

    def slot(self, s):
        return (self.at.z - s + TP) % TP

    def along_z(self, p, s):
        a = self.at
        return put(
            self.own[p], self.bufs[p].at[a.z, a.yx, a.cb], self.zs.at[p, s - 1], self.zr.at[p, s - 1], a.zdev(s)
        )

    def along_xy(self, p, s, j):
        a = self.at
        ref = self.bufs[p].at[self.slot(s), a.yx, a.cb]
        return put(ref, ref, self.ps.at[p, s, j], self.pr.at[p, s, j], (a.xn, a.yn)[j])

    def forward(self, p, s, j):
        a = self.at
        ref = self.bufs[p].at[self.slot(s), (a.x_yx, a.y_yx)[j], a.cb, pl.ds(j * 48, 48)]
        return put(ref, ref, self.ps.at[p, s, 2 + j], self.pr.at[p, s, 2 + j], (a.yn, a.xn)[j])

    def to_core(self, p, s):
        a = self.at
        ref = self.bufs[p].at[self.slot(s), :, a.cb]
        return put(ref, ref, self.ps.at[p, s, 4], self.pr.at[p, s, 4], a.core)

    def start_z(self, p):
        for s in (1, 2, 3):
            self.along_z(p, s).start()

    def tick(self):
        i, n = self.now, len(self.order)
        self.now += 1
        if i in ZPLAN:
            self.start_z(ZPLAN.index(i))
        for k in range(n):
            if max(k - AHEAD[k // 4], -1) == i:
                p, s = self.order[k]
                if s:
                    self.along_z(p, s).wait_recv()
                for j in (0, 1):
                    self.along_xy(p, s, j).start()
        if 0 <= i - 1 < n:
            p, s = self.order[i - 1]
            for j in (0, 1):
                self.along_xy(p, s, j).wait_recv()
                self.forward(p, s, j).start()
        if 0 <= i - 2 < n:
            p, s = self.order[i - 2]
            for j in (0, 1):
                self.forward(p, s, j).wait_recv()
            self.to_core(p, s).start()
        if 0 <= i - 3 < n:
            self.to_core(*self.order[i - 3]).wait_recv()

    def ready(self, p, s):
        while self.now <= self.order.index((p, s)) + 3:
            self.tick()

    def drain(self):
        self.ready(3, 3)
        for p, s in self.order:
            if s:
                self.along_z(p, s).wait_send()
            for j in (0, 1):
                self.along_xy(p, s, j).wait_send()
                self.forward(p, s, j).wait_send()
            self.to_core(p, s).wait_send()


def layer_norm(rows):
    center = rows - jnp.mean(rows, axis=-1, keepdims=True)
    spread = jnp.mean(center * center, axis=-1, keepdims=True)
    inverse = lax.rsqrt(spread + EPS)
    return center * inverse, inverse


def lanes(shape):
    return lax.broadcasted_iota(jnp.int32, shape, len(shape) - 1)


def halves(shape):
    return lanes(shape) < HD


def only(tile, left):
    keep = halves(tile.shape)
    return jnp.where(keep if left else jnp.logical_not(keep), tile.astype(F32), 0.0).astype(tile.dtype)


def gate_lane(head):
    return head if head < 3 else HD + head - 3


class Reduce:
    def __init__(self, at, produce, result, refs):
        self.at, self.produce, self.result = at, produce, result
        self.slots, self.rc, self.rh, self.rd, self.rz, self.ss, self.rs, self.zs, self.zr = refs
        self.order = [(p, s) for p in (3, 2, 1) for s in (1, 2, 3, 0)] + [(0, 1), (0, 2), (0, 3), (4, 0), (0, 0)]
        self.wide = COLS + (TILE,)
        self.off = OFF + (WIDE,)
        self.places = [0, 1, 2, 3] + list(range(5, 13)) + [0, 1, 2, 4, 3]
        self.now = 0
        self.done = [0, 0, 0]

    def slot(self, i):
        return (self.at.z + self.order[i][1]) % TP

    def width(self, i):
        return self.wide[self.order[i][0]]

    def copy(self, i, j, src, dst, device):
        return put(src, dst, self.ss.at[i, j], self.rs.at[i, j], device)

    def to_core(self, i):
        c = self.width(i)
        src = self.slots[i].at[:, 1 - self.at.cb, :, pl.ds(0, c)]
        return self.copy(i, 0, src, self.rc.at[i % 4, :, :, pl.ds(0, c)], self.at.core)

    def diagonal(self, i, j):
        a, c = self.at, self.width(i)
        src = self.slots[i].at[a.d_yx, a.cb, pl.ds(48 * j, 48), pl.ds(0, c)]
        return self.copy(i, 1 + j, src, self.rh.at[i % RING, j, :, pl.ds(0, c)], (a.xn, a.yn)[j])

    def direct(self, i, j):
        a, c = self.at, self.width(i)
        src = self.slots[i].at[(a.x_yx, a.y_yx)[j], a.cb, :, pl.ds(0, c)]
        return self.copy(i, 3 + j, src, self.rd.at[i % RING, j, :, pl.ds(0, c)], (a.xn, a.yn)[j])

    def along_z(self, i, far=None):
        a, (p, s) = self.at, self.order[i]
        s = far or s
        src = self.slots[i].at[a.yx, a.cb, :, pl.ds(0, self.wide[p])]
        return put(src, self.rz[p].at[s - 1], self.zs.at[p, s - 1], self.zr.at[p, s - 1], a.zdev(s))

    def to_z(self, i):
        p, s = self.order[i]
        return [self.along_z(i, far) for far in ((1, 2, 3) if p == 4 else (s,) if s else ())]

    def finish_sends(self, i):
        self.to_core(i).wait_send()
        for j in (0, 1):
            self.diagonal(i, j).wait_send()
            self.direct(i, j).wait_send()
        for copy in self.to_z(i):
            copy.wait_send()

    def tick(self):
        i = self.now
        self.now += 1
        for k in range(i):
            if self.places[k] == self.places[i]:
                self.finish_sends(k)
        self.produce(self.slots[i], *self.order[i], self.slot(i))
        self.to_core(i).start()
        self.move_on(LAG)

    def move_on(self, lag=(0, 0, 0)):
        for stage, step in enumerate((self.across, self.aside, self.home)):
            k = self.done[stage]
            before = self.done[stage - 1] if stage else self.now
            if k < before and k < self.now - lag[stage]:
                self.done[stage] += 1
                step(k)

    def across(self, k):
        a, c, w = self.at, self.width(k), self.slots[k]
        self.to_core(k).wait_recv()
        for q in (a.d_yx, a.x_yx, a.y_yx, a.yx):
            w[q, a.cb, :, 0:c] = (w[q, a.cb, :, 0:c].astype(F32) + self.rc[k % 4, q, :, 0:c].astype(F32)).astype(BF)
            if q is a.d_yx:
                for j in (0, 1):
                    self.diagonal(k, j).start()

    def aside(self, k):
        a, c, w = self.at, self.width(k), self.slots[k]
        for j in (0, 1):
            self.diagonal(k, j).wait_recv()
            q, rows = (a.y_yx, a.x_yx)[j], pl.ds(48 * j, 48)
            w[q, a.cb, rows, 0:c] = (
                w[q, a.cb, rows, 0:c].astype(F32) + self.rh[k % RING, j, :, 0:c].astype(F32)
            ).astype(BF)
            self.direct(k, 1 - j).start()

    def home(self, k):
        a, w = self.at, self.slots[k]
        p, s = self.order[k]
        c = self.wide[p]
        for j in (0, 1):
            self.direct(k, j).wait_recv()
        total = (
            w[a.yx, a.cb, :, 0:c].astype(F32)
            + self.rd[k % RING, 0, :, 0:c].astype(F32)
            + self.rd[k % RING, 1, :, 0:c].astype(F32)
        )
        if s or p == 4:
            w[a.yx, a.cb, :, 0:c] = total.astype(BF)
            for copy in self.to_z(k):
                copy.start()
        if not s:
            self.result[:, self.off[p] : self.off[p] + c] = total

    def finish(self):
        n = len(self.order)
        while self.now < n:
            self.tick()
        while self.done[2] < n:
            self.move_on()
        for i in range(4, n):
            self.finish_sends(i)
        for p in (3, 2, 1, 0, 4):
            for s in (1, 2, 3):
                self.along_z(self.order.index((p, 0 if p == 4 else s)), s).wait_recv()
            lo, c = self.off[p], self.wide[p]
            self.result[:, lo : lo + c] += (
                self.rz[p][0].astype(F32) + self.rz[p][1].astype(F32) + self.rz[p][2].astype(F32)
            )


def norm_back(grad, normed, inverse, gain):
    inner = grad * gain
    return inverse * (
        inner - jnp.mean(inner, -1, keepdims=True) - normed * jnp.mean(inner * normed, -1, keepdims=True)
    )


def layer_kernel(
    inner, tok, cot, w_qkv, score_rows, w_out, w_fc, proj_rows, one, two, sel, holder,
    out_h, gin_h, grads, pt_h,
    ga, gb, gc, gd, pack, first, mixed, mrecv, sg, selz, selp, selq, selrow, kvp, kvc, qp, qc, gp, sb, oh, bias, atpc,
    att, resid, second, hid, dg, gwt, gains, wide, xt0, xt1, gattr, acc, gacc, dsel, come, gaway, gcome, cols,
    w, rc, rh, rd, rz0, rz1, rz2, rz3, rz4,
    zs, zr, ps, pr, es, er, ls, ss, rs, rzs, rzr,
):
    at = Place(inner)
    bufs = (ga, gb, gc, gd)
    own = [pack.at[:, pl.ds(OFF[p], COLS[p])] for p in range(4)]
    g = Gather(at, own, bufs, (zs, zr, ps, pr))
    atp, atc, gm, gs = atpc.at[0], atpc.at[1], mixed, mrecv
    odd = at.z % 2
    tiles = [slice(128 * k, 128 * k + 128) for k in range(6)]

    def flipped(dst, src):
        for r in range(0, ROWS, 128):
            for cut in tiles:
                dst[cut, r : r + 128] = src[r : r + 128, cut].astype(F32).T.astype(BF)

    is_odd = lanes((96, TILE)) * 0 + odd == 1
    q0, k0, v0, q1, k1, v1, q2, k2, v2 = [w_qkv[:, 64 * k : 64 * k + 64].astype(F32) for k in range(9)]
    rowed = jnp.concatenate([score_rows[...].astype(F32), one[...].astype(F32), two[...].astype(F32)], 0)
    rowed = jnp.concatenate([rowed, jnp.zeros((5, 32), F32)], 1)
    extra = jnp.concatenate([rowed, jnp.zeros((TILE - 5, TILE), F32)], 0).T[0:96, 0:HD]
    even_cols = ((v0, k0), (k1, v1), (v2, k2), (q1, q0), (extra, q2))
    odd_cols = ((k0, v0), (v1, k1), (k2, v2), (q2, q1), (q0, extra))
    for k in range(5):
        tile = jnp.where(is_odd, jnp.concatenate(odd_cols[k], 1), jnp.concatenate(even_cols[k], 1)).astype(BF)
        pack[:, tiles[k]] = tile
        ga[at.z, at.yx, at.cb, :, tiles[k]] = tile
    at.barrier()
    g.start_z(0)
    g.tick()

    def blocks_of(z):
        return pl.ds(pl.multiple_of(8 * z, 8), 8)

    selz[at.z] = sel[:, blocks_of(at.z), :]
    sel_out = [
        put(sel.at[:, blocks_of((at.z + s) % TP)], selz.at[at.z], es.at[s - 1], er.at[s - 1], at.zdev(s)) for s in (1, 2, 3)
    ]
    for copy in sel_out:
        copy.start()
    flipped_out = jnp.concatenate([w_out[...].astype(F32), jnp.zeros((64, 96), F32)], 0)
    pack[:, 640:896] = flipped_out.T.astype(BF)
    pack[:, 896:1664] = w_fc[...]
    pack[:, 1664:2432] = proj_rows[...]
    for p in (1, 2, 3):
        bufs[p][at.z, at.yx, at.cb] = own[p][...]
    g.tick()
    f = jnp.full((1, TILE), jnp.where(holder[at.dp // 2 * 2 + at.z // 2] == at.c, 1.0, 0.0), F32)
    fb = f.astype(BF)
    nb = (1.0 - f).astype(BF)

    key = lax.broadcasted_iota(jnp.int32, (256, TILE), 0)
    row = lax.broadcasted_iota(jnp.int32, (256, TILE), 1)
    gap = row + TILE - key
    band = (gap >= 0) & (gap < HD)
    bias[0] = jnp.where(band, 0.0, FAR_OFF)
    reach = TILE * (1 - at.half)
    bias[1] = jnp.where(band & (key >= reach), 0.0, FAR_OFF)
    close = (row - key >= 0) & (row - key < HD)
    bias[2] = jnp.where(
        ((key < TILE) & close) | ((key >= TILE) & ((key - TILE) // HD == row // HD)), 0.0, FAR_OFF
    )
    kvp[:, 0:TILE, :] = jnp.zeros((6, TILE, TILE), BF)

    normed = layer_norm(tok[...].astype(F32))[0]
    for copy in sel_out:
        copy.wait()
    sel_core = put(selz.at[pl.ds(2 * (1 - at.c), 2)], selp, es.at[3], er.at[3], at.pair)
    sel_core.start()
    flipped(xt0, cot)
    g.ready(0, 0)
    extra = ga[at.z, :, :, :, 512:640].reshape(D, TILE).astype(F32).T
    odd_f = odd.astype(F32)
    gains[...] = extra[0:8] * (1.0 - odd_f) + extra[HD : HD + 8] * odd_f
    gain_one, gain_two = gains[3:4, :], gains[4:5, :]
    first[...] = (normed * gain_one).astype(BF)
    sel_core.wait()
    fi = f.astype(jnp.int32)[:, 0:64]
    columns = []
    for i in range(2):
        for j in range(3):
            selq[i, 8 * j : 8 * j + 8, :] = selz[2 * at.c + i, j] * (1 - fi) + selp[i, j] * fi
        both = selq[i]
        square = jnp.concatenate([both.astype(F32), jnp.zeros((104, HD), F32)], 0)
        columns.append(jnp.concatenate([square, jnp.zeros((TILE, HD), F32)], 1).T.astype(jnp.int32))
        for r in range(12):
            selrow[i, r : r + 1, :] = jnp.concatenate([both[2 * r : 2 * r + 1, :], both[2 * r + 1 : 2 * r + 2, :]], 1)

    for s in range(TP):
        g.ready(0, s)
        t = g.slot(s)
        weight = ga[t].reshape(D, 640)
        extra_side = (lanes((256, TILE)) // HD) == t % 2
        for r in range(0, ROWS, 256):
            got = nn(first[r : r + 256, :], weight)
            mixed[t, r : r + 256, 0:512] = got[:, 0:512].astype(BF)
            last = got[:, 512:640]
            soft_part = jnp.log(1.0 + jnp.exp(-jnp.abs(last)))
            mixed[t, r : r + 256, 512:640] = jnp.where(
                extra_side, jnp.minimum(last, 0.0) - soft_part, last
            ).astype(BF)
            sg[t, r : r + 256, :] = (1.0 / (1.0 + jnp.exp(last))).astype(BF)
    swap = [
        put(mixed.at[2 * (1 - at.c) + i], mrecv.at[i], es.at[4 + i], er.at[4 + i], at.pair) for i in range(2)
    ]
    for copy in swap:
        copy.start()
    g.tick()
    for copy in swap:
        copy.wait()
    base = pl.multiple_of(TILE + ROWS * at.half, TILE)
    other = pl.multiple_of(TILE + ROWS * (1 - at.half), TILE)
    gate_base = pl.multiple_of(ROWS * at.half, ROWS)
    left = halves((ROWS, TILE))
    gate_own = jnp.where(left, mixed[2 * at.c, :, 512:640].astype(F32), mixed[2 * at.c + 1, :, 512:640].astype(F32))
    gate_pair = jnp.where(left, mrecv[0, :, 512:640].astype(F32), mrecv[1, :, 512:640].astype(F32))
    wanted = (lanes((ROWS, TILE)) % HD) < 3
    gp[pl.ds(gate_base, ROWS), :] = jnp.where(wanted, gate_own * f + gate_pair * (1.0 - f), 0.0).astype(BF)
    part = gp.at[pl.ds(gate_base, ROWS)]
    over = [put(part, part, es.at[6], er.at[6], at.zp)]
    over[0].start()
    for i in range(2):
        for j in range(3):
            a = mixed[2 * at.c + i, :, tiles[j]]
            b = mrecv[i, :, tiles[j]]
            h = 3 * i + j
            kvp[h, pl.ds(base, ROWS), :] = a * fb + b * nb
            part = kvp.at[h, pl.ds(base, ROWS)]
            over.append(put(part, part, es.at[7 + h], er.at[7 + h], at.zp))
            over[-1].start()
            kvc[h] = a * nb + b * fb
    for n in range(3):
        if n == 1:
            a = jnp.where(left, mixed[2 * at.c + 1, :, 512:640].astype(F32), mixed[2 * at.c, :, 512:640].astype(F32)).astype(BF)
            b = jnp.where(left, mrecv[1, :, 512:640].astype(F32), mrecv[0, :, 512:640].astype(F32)).astype(BF)
        else:
            a = mixed[2 * at.c + n // 2, :, 384:512]
            b = mrecv[n // 2, :, 384:512]
        eighth = jnp.asarray(0.125, BF)
        qp[n] = (a * fb + b * nb) * eighth
        qc[n] = (a * nb + b * fb) * eighth
    g.tick()

    low_lanes = halves((TILE, TILE))

    def soft(scores, table):
        scores = scores + table
        top = jnp.max(scores, axis=0, keepdims=True)
        raised = jnp.exp(scores - top)
        return (raised * (1.0 / jnp.sum(raised, axis=0, keepdims=True))).astype(BF)

    def shares_at(h, tile):
        return tile // 2, slice(tile % 2 * 256, tile % 2 * 256 + 256), tiles[h]

    def near_keys(h, tau):
        return kvp[h, pl.ds(pl.multiple_of(ROWS * at.half + TILE * tau, TILE), 256), :]

    def far_keys(h, tau):
        return jnp.concatenate([kvc[h, tiles[tau], :], sb[h, tiles[tau], 0:TILE]], 0)

    def hot_lane(h):
        return jnp.where(lanes((TILE, TILE)) == gate_lane(h), 1.0, 0.0).astype(BF)

    def attend(n, taus, far, table):
        done = []
        for tau in taus:
            q = (qc if far else qp)[n, tiles[tau], :]
            for par in range(2):
                h = 2 * n + par
                query = only(q, par == 1)
                if far:
                    kv = far_keys(h, tau)
                    gate = jnp.concatenate([jnp.zeros((TILE, TILE), BF), sb[h, tiles[tau], TILE : 2 * TILE]], 0)
                    scores = nt(jnp.concatenate([kv, gate], 1), jnp.concatenate([query, hot_lane(h)], 1))
                else:
                    kv = near_keys(h, tau)
                    scores = nt(kv, query)
                shares = soft(scores, table)
                done.append((h, tau, shares, tn(shares, kv)))
        for k, (h, tau, shares, got) in enumerate(done):
            hid[shares_at(h, tau + (4 if far else 0))] = shares
            if h % 2:
                (atc if far else atp)[n, tiles[tau], :] = jnp.where(low_lanes, done[k - 1][3], got).astype(BF)

    def pick(h):
        for tau in range(4):
            r = 8 * (h % 3) + 2 * tau
            cut = columns[h // 3]
            col = jnp.concatenate(
                [jnp.broadcast_to(cut[0:HD, r + k : r + k + 1], (HD, TILE)) for k in range(2)], 0
            )
            for k in range(8):
                oh[tiles[tau], 128 * k : 128 * k + 128] = jnp.where(col == lanes((TILE, TILE)) + 128 * k, 1.0, 0.0).astype(BF)
        table = jnp.concatenate([kvp[h, TILE : TILE + UNIT, :], gp[...]], 1)
        for r in range(0, ROWS, 256):
            sb[h, r : r + 256, :] = nn(oh[r : r + 256, :], table).astype(BF)

    for n in range(3):
        attend(n, (1, 2, 3), False, bias[0])
        g.tick()
    while g.now < EARLY:
        g.tick()
    over[0].wait()
    for n in range(3):
        for par in range(2):
            over[1 + 2 * n + par].wait()
        attend(n, (0,), False, bias[1])
        for par in range(2):
            pick(2 * n + par)
        attend(n, (0, 1, 2, 3), True, bias[2])
        g.tick()
    pt_save = pltpu.make_async_copy(hid, pt_h, ls.at[0])
    pt_save.start()

    for n in range(3):
        a, b = atp[n], atc[n]
        att[at.c, n] = a * fb + b * nb
        atp[n] = a * nb + b * fb
    back = put(atp, att.at[at.c], es.at[13], er.at[13], at.pair)
    back.start()
    g.ready(1, 3)
    gwt[...] = jnp.concatenate([gb[t].reshape(D, 256)[:, 0:192] for t in range(TP)], 1)
    back.wait()
    for r in range(0, ROWS, 256):
        branch = nt(
            jnp.concatenate([att[k, n, r : r + 256, :] for k in range(2) for n in range(3)], 1), gwt[...]
        )
        kept = tok[r : r + 256, :].astype(F32) + branch
        resid[r : r + 256, :] = kept
        low = (layer_norm(kept)[0] * gain_two).astype(BF)
        second[r : r + 256, :] = low
        for q in (r, r + 128):
            for cut in tiles:
                xt1[cut, q : q + 128] = low[q - r : q - r + 128, cut].astype(F32).T.astype(BF)
    pt_save.wait()

    def produce(slot, p, s, t):
        lhs = (xt1, xt0, xt1, xt0)[p] if p < 4 else None
        if p == 3:
            rhs = hid[t]
        elif p == 2:
            rhs = dg[t]
        elif p == 0:
            rhs = gm[t]
        elif p == 1:
            whole = jnp.concatenate([att[k, n] for k in range(2) for n in range(3)], 1)
            rhs = jnp.concatenate([whole[:, 0:192], jnp.zeros((ROWS, 64), BF)], 1)
            for o in range(1, 4):
                cut = jnp.concatenate([whole[:, 192 * o : 192 * o + 192], jnp.zeros((ROWS, 64), BF)], 1)
                rhs = jnp.where(t == o, cut, rhs)
        for k in range(8):
            block = cols[96 * k : 96 * k + 96, :] if p == 4 else nn(lhs[96 * k : 96 * k + 96, :], rhs)
            slot[k // 2, k % 2, :, 0 : block.shape[1]] = block.astype(BF)

    slots = [ref.at[k] for ref in (w, gd, gc) for k in range(4)] + [w.at[k] for k in (0, 1, 2, 4, 3)]
    red = Reduce(at, produce, grads, (slots, rc, rh, rd, (rz0, rz1, rz2, rz3, rz4), ss, rs, rzs, rzr))

    for s in range(TP):
        g.ready(2, s)
        t = g.slot(s)
        weight = gc[t].reshape(D, 768)
        for r in range(0, ROWS, 256):
            v = nn(second[r : r + 256, :], weight)
            square = v * v
            th = jnp.tanh(GELU * (v + CUBE * v * square))
            half = 0.5 * (1.0 + th)
            hid[t, r : r + 256, :] = (v * half).astype(BF)
            slope_of = half + 0.5 * v * (1.0 - th * th) * (GELU * (1.0 + 3.0 * CUBE * square))
            dg[t, r : r + 256, :] = slope_of.astype(BF)
    for s in range(TP):
        red.tick()
        g.ready(3, s)
        t = g.slot(s)
        weight = gd[t].reshape(D, 768)
        for r in range(0, ROWS, 256):
            rows = slice(r, r + 256)
            wide[rows, :] = (resid if s == 0 else wide)[rows, :] + nt(hid[t, rows, :], weight)
            got = nn(cot[rows, :], weight)
            dg[t, rows, :] = (got * dg[t, rows, :].astype(F32)).astype(BF)
    out_save = pltpu.make_async_copy(wide, out_h, ls.at[1])
    out_save.start()
    pt_load = pltpu.make_async_copy(pt_h, hid, ls.at[2])
    pt_load.start()
    g.drain()
    out_save.wait()
    for t in range(TP):
        for r in range(0, ROWS, 256):
            rows = slice(r, r + 256)
            got = nt(dg[t, rows, :], gc[t].reshape(D, 768))
            wide[rows, :] = got if t == 0 else wide[rows, :] + got
    part_two = jnp.zeros((1, D), F32)
    for r in range(0, ROWS, 128):
        rows = slice(r, r + 128)
        got = wide[rows, :]
        normed, inverse = layer_norm(resid[rows, :])
        part_two += jnp.sum(got * normed, 0, keepdims=True)
        grad_back = cot[rows, :].astype(F32) + norm_back(got, normed, inverse, gain_two)
        wide[rows, :] = grad_back
        low = grad_back.astype(BF)
        second[rows, :] = low
        for cut in tiles:
            xt0[cut, rows] = grad_back[:, cut].T.astype(BF)
    gatt = atpc
    for r in range(0, ROWS, 256):
        grad_att = nn(second[r : r + 256, :], gwt[...]).astype(BF)
        for k in range(2):
            for n in range(3):
                gatt[k, n, r : r + 256, :] = grad_att[:, tiles[3 * k + n]]
    swap = put(gatt.at[1 - at.c], gattr, es.at[14], er.at[14], at.pair)
    swap.start()
    gacc[...] = jnp.zeros_like(gacc)
    red.tick()
    pt_load.wait()
    swap.wait()
    for n in range(3):
        a, b = gatt[at.c, n], gattr[n]
        gatt[at.c, n] = a * fb + b * nb
        gattr[n] = a * nb + b * fb

    over = []

    def slope(shares, kv, up):
        spread = nt(kv, up)
        p = shares.astype(F32)
        prod = p * spread
        return (prod - p * jnp.sum(prod, 0, keepdims=True)).astype(BF)

    def far_back(n):
        done = []
        for tau in range(4):
            q, up_pair = qc[n, tiles[tau], :], gattr[n, tiles[tau], :]
            for par in range(2):
                h = 2 * n + par
                kv = far_keys(h, tau)
                up = only(up_pair, par == 0)
                shares = hid[shares_at(h, 4 + tau)]
                down = slope(shares, kv, up)
                rhs = jnp.concatenate(
                    [jnp.concatenate([only(q, par == 1), hot_lane(h)], 1), jnp.concatenate([up, jnp.zeros_like(up)], 1)], 0
                )
                done.append((h, tau, nn(jnp.concatenate([down, shares], 1), rhs), tn(down, kv)))
        for k, (h, tau, grad, dq) in enumerate(done):
            kvc[h, tiles[tau], :] = grad[0:TILE, 0:TILE].astype(BF)
            dsel[h % 2, tiles[tau], :] = grad[TILE:256, :].astype(BF)
            if h % 2:
                qc[n, tiles[tau], :] = (jnp.where(low_lanes, dq, done[k - 1][3]) * 0.125).astype(BF)

    def near_back(n):
        done = []
        for tau in range(4):
            q, up_pair = qp[n, tiles[tau], :], gatt[at.c, n, tiles[tau], :]
            for par in range(2):
                h = 2 * n + par
                kv = near_keys(h, tau)
                up = only(up_pair, par == 0)
                shares = hid[shares_at(h, tau)]
                down = slope(shares, kv, up)
                grad = nn(jnp.concatenate([down, shares], 1), jnp.concatenate([only(q, par == 1), up], 0))
                done.append((h, tau, grad, tn(down, kv)))
        for k, (h, tau, grad, dq) in enumerate(done):
            start = pl.multiple_of(ROWS * at.half + TILE * tau, TILE)
            acc[h % 2, pl.ds(start, 256), :] += grad
            if h % 2:
                qp[n, tiles[tau], :] = (jnp.where(low_lanes, dq, done[k - 1][3]) * 0.125).astype(BF)

    def scatter(h):
        for tau in range(4):
            r = (h % 3) * 4 + tau
            chosen = jnp.broadcast_to(selrow[h // 3, r : r + 1, :], (TILE, TILE))
            for k in range(8):
                oh[tiles[k % 4], 512 * (k // 4) + 128 * tau : 512 * (k // 4) + 128 * tau + 128] = jnp.where(
                    chosen == lax.broadcasted_iota(jnp.int32, (TILE, TILE), 0) + 128 * k, 1.0, 0.0
                ).astype(BF)
        acc[h % 2, 0:TILE, :] = jnp.zeros((TILE, TILE), F32)
        for r in range(0, UNIT, 256):
            got = nn(oh[r % 512 : r % 512 + 256, 512 * (r // 512) : 512 * (r // 512) + 512], dsel[h % 2])
            acc[h % 2, TILE + r : TILE + r + 256, :] = got[:, 0:TILE]
            gacc[r : r + 256, :] += got[:, TILE : 2 * TILE]

    for n in range(3):
        far_back(n)
        red.tick()
        for par in range(2):
            scatter(2 * n + par)
        near_back(n)
        for par in range(2):
            h = 2 * n + par
            kvp[h, pl.ds(other, ROWS), :] = acc[par, pl.ds(other, ROWS), :].astype(BF)
            kvp[h, pl.ds(base, ROWS), :] = acc[par, pl.ds(base, ROWS), :].astype(BF)
            over.append(put(kvp.at[h, pl.ds(other, ROWS)], come.at[h], es.at[15 + h], er.at[15 + h], at.zp))
            over[-1].start()
        red.tick()
    gaway[...] = gacc[pl.ds(pl.multiple_of(ROWS * (1 - at.half), ROWS), ROWS), :].astype(BF)
    over.append(put(gaway, gcome, es.at[21], er.at[21], at.zp))
    over[-1].start()
    while red.now < LATE:
        red.tick()
    for _ in range(PUSH):
        red.move_on()
    for copy in over:
        copy.wait()
    gate = gacc[pl.ds(gate_base, ROWS), :] + gcome[...].astype(F32)

    def deal(i, lo, a, b):
        gm[2 * at.c + i, :, lo : lo + 128] = a * fb + b * nb
        gs[i, :, lo : lo + 128] = a * nb + b * fb

    for h in range(6):
        total = kvp[h, pl.ds(base, ROWS), :].astype(F32) + come[h].astype(F32)
        deal(h // 3, 128 * (h % 3), total.astype(BF), kvc[h])
    deal(0, 384, qp[0], qc[0])
    deal(1, 384, qp[2], qc[2])
    zero = jnp.zeros((ROWS, TILE), F32)
    middle, middle_c = qp[1].astype(F32), qc[1].astype(F32)
    deal(0, 512, jnp.where(left, gate, middle).astype(BF), jnp.where(left, zero, middle_c).astype(BF))
    deal(1, 512, jnp.where(left, middle, gate).astype(BF), jnp.where(left, middle_c, zero).astype(BF))
    swap = [put(gs.at[i], gm.at[2 * at.c + i], es.at[22 + i], er.at[22 + i], at.pair) for i in range(2)]
    for copy in swap:
        copy.start()
    while red.now < 12:
        red.tick()
    flipped(xt1, first)
    for copy in swap:
        copy.wait()
    for t in range(TP):
        side = left if t % 2 == 0 else jnp.logical_not(left)
        last = gm[t, :, 512:640].astype(F32)
        gm[t, :, 512:640] = jnp.where(side, last * sg[t].astype(F32), last).astype(BF)
    for t in range(TP):
        if t < 3:
            red.tick()
        for r in range(0, ROWS, 256):
            rows = slice(r, r + 256)
            got = nt(gm[t, rows, :], ga[t].reshape(D, 640))
            resid[rows, :] = got if t == 0 else resid[rows, :] + got
    part_one = jnp.zeros((1, D), F32)
    for r in range(0, ROWS, 128):
        rows = slice(r, r + 128)
        got = resid[rows, :]
        normed, inverse = layer_norm(tok[rows, :].astype(F32))
        part_one += jnp.sum(got * normed, 0, keepdims=True)
        wide[rows, :] += norm_back(got, normed, inverse, gain_one)
    gin_save = pltpu.make_async_copy(wide, gin_h, ls.at[3])
    gin_save.start()
    cols[...] = jnp.concatenate([part_one, part_two, jnp.zeros((TILE - 2, D), F32)], 0).T
    red.finish()
    gin_save.wait()


def layer(tok, cot, w_qkv, score_rows, w_out, w_fc, proj_rows, one, two, sel, holder, inner):
    dma = pltpu.SemaphoreType.DMA
    V = pltpu.VMEM
    vm = pl.BlockSpec(memory_space=pltpu.VMEM)
    anyw = pl.BlockSpec(memory_space=pl.ANY)
    wide = V((TP, ROWS, 768), BF)
    sq, flip = V((ROWS, D), BF), V((D, ROWS), BF)
    three, six = V((3, ROWS, TILE), BF), V((6, ROWS, TILE), BF)
    picks = V((2, 24, HD), jnp.int32)
    scratch = [V((TP, 4, 2, 96, c), BF) for c in COLS] + [
        V((96, WIDE), BF), sq, V((TP, ROWS, 640), BF), V((2, ROWS, 640), BF), V((TP, ROWS, TILE), BF),
        V((TP, 3, 8, HD), jnp.int32), V((2, 3, 8, HD), jnp.int32), picks, V((2, 16, TILE), jnp.int32),
        V((6, TILE + UNIT, TILE), BF), six, three, three, V((UNIT, TILE), BF), V((6, ROWS, 2 * TILE), BF),
        V((ROWS, UNIT), BF), V((3, 256, TILE), F32), V((2, 3, ROWS, TILE), BF),
        V((2, 3, ROWS, TILE), BF), V((ROWS, D), F32), sq, wide, wide, V((D, D), BF), V((8, D), F32), V((ROWS, D), F32),
        flip, flip, three, V((2, TILE + UNIT, TILE), F32), V((UNIT, TILE), F32), V((2, ROWS, 2 * TILE), BF), six,
        V((ROWS, TILE), BF), V((ROWS, TILE), BF), V((D, TILE), F32),
        V((5, 4, 2, 96, 768), BF), V((4, 4, 96, 768), BF), V((RING, 2, 48, 768), BF), V((RING, 2, 96, 768), BF),
    ] + [V((3, 96, c), BF) for c in COLS + (TILE,)] + [
        dma((4, 3)), dma((4, 3)), dma((4, 4, 5)), dma((4, 4, 5)), dma((24,)), dma((24,)), dma((4,)),
        dma((17, 5)), dma((17, 5)), dma((5, 3)), dma((5, 3)),
    ]
    return pl.pallas_call(
        functools.partial(layer_kernel, inner),
        out_shape=[
            jax.ShapeDtypeStruct((ROWS, D), F32), jax.ShapeDtypeStruct((ROWS, D), F32),
            jax.ShapeDtypeStruct((96, ALL), F32), jax.ShapeDtypeStruct((TP, ROWS, 768), BF),
        ],
        in_specs=[vm] * 10 + [pl.BlockSpec(memory_space=pltpu.SMEM)],
        out_specs=[anyw, anyw, vm, anyw],
        scratch_shapes=scratch,
        compiler_params=pltpu.CompilerParams(collective_id=0, has_side_effects=True, vmem_limit_bytes=64 << 20),
    )(tok, cot, w_qkv, score_rows, w_out, w_fc, proj_rows, one, two, sel, holder)


EVEN = (7, 1, 0, 6, 2, 3, 9, 5, 4)
ODD = (8, 0, 1, 7, 3, 2, 6, 4, 5)


def finish_kernel(out_h, gin_h, grads, out, gin, qkv, score, w_out, fc, proj, one, two, sems):
    copies = [pltpu.make_async_copy(a, b, sems.at[k]) for k, (a, b) in enumerate(((out_h, out), (gin_h, gin)))]
    for copy in copies:
        copy.start()
    odd = lax.axis_index("tp") % 2
    is_odd = lanes((96, HD)) * 0 + odd == 1
    piece = [grads[:, 64 * k : 64 * k + 64] for k in range(10)]
    for k in range(9):
        qkv[:, 64 * k : 64 * k + 64] = jnp.where(is_odd, piece[ODD[k]], piece[EVEN[k]])
    extra = jnp.concatenate([jnp.where(is_odd, piece[9], piece[8]), grads[:, WIDE : WIDE + HD]], 1)
    score[...] = jnp.concatenate([extra, jnp.zeros((32, TILE), F32)], 0).T[0:3, 0:96]
    fc[...] = grads[:, 896:1664]

    def turned(lo, hi):
        return jnp.concatenate([grads[:, lo:hi], jnp.zeros((32, hi - lo), F32)], 0).T[:, 0:96]

    w_out[...] = turned(640, 896)[0:192, :]
    proj[...] = grads[:, 1664:2432]
    gain = turned(WIDE, ALL)
    one[...] = gain[0:1, :]
    two[...] = gain[1:2, :]
    for copy in copies:
        copy.wait()


def finished(out, grad_in, grads):
    vm = pl.BlockSpec(memory_space=pltpu.VMEM)
    anyw = pl.BlockSpec(memory_space=pl.ANY)
    shapes = ((ROWS, D), (ROWS, D), (96, 576), (3, 96), (192, 96), (96, 768), (96, 768), (1, 96), (1, 96))
    got = pl.pallas_call(
        finish_kernel,
        out_shape=[jax.ShapeDtypeStruct(s, F32) for s in shapes],
        in_specs=[vm] * 3,
        out_specs=[anyw, anyw] + [vm] * 7,
        scratch_shapes=[pltpu.SemaphoreType.DMA((2,))],
        compiler_params=pltpu.CompilerParams(vmem_limit_bytes=60 << 20),
    )(out, grad_in, grads)
    out, gin, qkv, score, w_out, fc, proj, one, two = got
    return out, gin, qkv, score.T, w_out, fc, proj.T, one.reshape(96), two.reshape(96)


def unpacked(grads):
    odd = lax.axis_index("tp") % 2 == 1
    piece = [grads[:, 64 * k : 64 * k + 64] for k in range(10)]
    qkv = jnp.where(
        odd, jnp.concatenate([piece[k] for k in ODD], 1), jnp.concatenate([piece[k] for k in EVEN], 1)
    )
    extra = jnp.where(odd, piece[9], piece[8])
    return (
        qkv, extra[:, 0:3], grads[:, 640:832].T, grads[:, 896:1664], grads[:, 1664:2432].T, grads[:, WIDE], grads[:, WIDE + 1]
    )


def per_device(
    tokens, w_qkv, w_score, w_out, w_fc, w_proj, ln1_gain, ln2_gain, selected, holder, cotangent
):
    inner = lax.axis_size("dp") // 8
    one, two = ln1_gain.reshape(1, -1), ln2_gain.reshape(1, -1)
    score_rows, proj_rows = w_score.T, w_proj.T
    groups = [[o * inner + i for i in range(inner)] for o in range(8)]
    if inner > 1:
        def whole(block, axis):
            return lax.all_gather(block, "dp", axis=axis, tiled=True, axis_index_groups=groups)

        w_qkv, w_fc = whole(w_qkv, 0), whole(w_fc, 0)
        w_out, proj_rows, score_rows, one, two = (
            whole(w_out, 1), whole(proj_rows, 0), whole(score_rows, 1), whole(one, 1), whole(two, 1)
        )
    out, grad_in, grads, _ = layer(
        tokens, cotangent, w_qkv, score_rows, w_out, w_fc, proj_rows, one, two, selected.transpose(1, 0, 2), holder, inner
    )
    if inner == 1:
        return finished(out, grad_in, grads)
    grads = lax.psum_scatter(grads, "dp", scatter_dimension=0, tiled=True, axis_index_groups=groups)
    return (out, grad_in) + unpacked(grads)


def solution(mesh):
    rows = P(("dp", "tp"), None)
    cols, flip = P("dp", "tp"), P("tp", "dp")
    return jax.shard_map(
        per_device,
        mesh=mesh,
        in_specs=(rows, cols, cols, flip, cols, flip, P("dp"), P("dp"), P("dp", "tp", None), P(), rows),
        out_specs=(rows, rows, cols, cols, flip, cols, flip, P("dp"), P("dp")),
        check_vma=False,
    )
```
